256 devices in a mesh: bl: 32 (over x, y, core), ch: 8 (over z).
Axes of the slice: x: 4, y: 4, z: 8, core: 2. Of those that a mesh axis runs over, the one named last changes fastest.
Arguments:
- visibilities: float32 [8, 32, 16384], P(None, 'ch', 'bl'), may hold values from -24 to 24
- model: bfloat16 [8, 8, 32, 16384], P(None, None, 'ch', 'bl'), may hold values from -6 to 6
- first_station: int32 [16384], P('bl'), may hold values from 0 to 511
- second_station: int32 [16384], P('bl'), may hold values from 0 to 511
- gain_offset: float32 [8, 8, 32, 512], P(None, None, 'ch', 'bl'), may hold values from -1.5 to 1.5
Outputs:
- smoothed: float32 [8, 8, 32, 512], P(None, None, 'ch', 'bl')
- misfit: float32 [3], replicated
The draws below stay inside these ranges and needn't reach their ends.
All inputs are finite; a program needn't handle non-finite values.
Results may differ from the reference program's by a relative error of at most 0.0003.
Values sent between devices are 32-bit elements; how exact they have to be, the bound alone decides.
A program may use at most 128 MiB of HBM per device.

```python
import jax
import jax.numpy as jnp
from jax import lax

STATION_COUNT = 512
DIRECTION_COUNT = 8
ITERS = 3
SPAN = 4
BASELINE_TOTAL = 16384
CHANNEL_COUNT = 32


def with_ends(result, own_key, low, top_value):
    spot = [jax.random.randint(jax.random.fold_in(own_key, axis), (), 0, length) for axis, length in enumerate(result.shape)]
    widest = result.shape.index(max(result.shape))
    next_to = spot[:widest] + [(spot[widest] + 1) % result.shape[widest]] + spot[widest + 1:]
    return result.at[tuple(spot)].set(low).at[tuple(next_to)].set(top_value)


def level_of(own_key, dims, shards, smallest, largest):
    def one(position, parts):
        heights = jax.random.uniform(jax.random.fold_in(jax.random.fold_in(own_key, 6), position), (parts,), jnp.float32, smallest / len(shards), largest / len(shards))
        return jnp.repeat(jnp.exp(heights), dims[position] // parts).reshape((-1,) + (1,) * (len(dims) - position - 1))

    level = one(*shards[0])
    for cut in shards[1:]:
        level = level * one(*cut)
    return level


def normal_values(stream_key, dims, deviation, reach, split=(), kind=jnp.bfloat16):
    drawn = jax.random.normal(stream_key, dims, jnp.float32) * deviation
    if len(split) > 0:
        drawn = level_of(stream_key, dims, split, -0.22, 0.18) * drawn
    return jnp.clip(drawn, min=-reach, max=reach).astype(kind)


def setup_inputs(seed: int = 0) -> dict:
    streams_of = jax.random.split(jax.random.key(seed), 6)
    return {
        "visibilities": normal_values(streams_of[0], (8, CHANNEL_COUNT, BASELINE_TOTAL), 3.0, 24.0, ((1, 8), (2, 32)), jnp.float32),
        "model": normal_values(streams_of[1], (DIRECTION_COUNT, 8, CHANNEL_COUNT, BASELINE_TOTAL), 1.0, 6.0, ((2, 8), (3, 32))),
        "first_station": with_ends(jax.random.randint(streams_of[2], (BASELINE_TOTAL,), 0, STATION_COUNT), jax.random.fold_in(streams_of[2], 1), 0, STATION_COUNT - 1).astype(jnp.int32),
        "second_station": with_ends(jax.random.randint(streams_of[3], (BASELINE_TOTAL,), 0, STATION_COUNT), jax.random.fold_in(streams_of[3], 1), 0, STATION_COUNT - 1).astype(jnp.int32),
        "gain_offset": normal_values(streams_of[4], (DIRECTION_COUNT, 8, CHANNEL_COUNT, STATION_COUNT), 0.3, 1.5, ((2, 8), (3, 32)), jnp.float32),
    }


REG = 1.0
KERNEL_VAR = 4.0


def split22(x):
    return [(x[:, 2 * k], x[:, 2 * k + 1]) for k in range(4)]


def join22(m):
    return jnp.stack([m[k][j] for k in range(4) for j in range(2)], axis=1)


def cmul(a, b):
    return (a[0] * b[0] - a[1] * b[1], a[0] * b[1] + a[1] * b[0])


def cadd(a, b):
    return (a[0] + b[0], a[1] + b[1])


def conj(a):
    return (a[0], -a[1])


def matmul22(a, b):
    return [cadd(cmul(a[0], b[0]), cmul(a[1], b[2])), cadd(cmul(a[0], b[1]), cmul(a[1], b[3])),
            cadd(cmul(a[2], b[0]), cmul(a[3], b[2])), cadd(cmul(a[2], b[1]), cmul(a[3], b[3]))]


def herm(a):
    return [conj(a[0]), conj(a[2]), conj(a[1]), conj(a[3])]


def gram_parts(y):
    diag_one = y[0][0] ** 2 + y[0][1] ** 2 + y[1][0] ** 2 + y[1][1] ** 2
    diag_two = y[2][0] ** 2 + y[2][1] ** 2 + y[3][0] ** 2 + y[3][1] ** 2
    off = cadd(cmul(y[0], conj(y[2])), cmul(y[1], conj(y[3])))
    return jnp.stack([diag_one, diag_two, off[0], off[1]], axis=1)


def station_terms(gain_p, gain_q, model, visibilities):
    mod = split22(model.astype(jnp.float32))
    jones_p = split22(gain_p)
    jones_q = split22(gain_q)
    y_one = matmul22(mod, herm(jones_q))
    pred_parts = matmul22(jones_p, y_one)
    y_two = matmul22(herm(mod), herm(jones_p))
    pred = join22(pred_parts)
    resid = visibilities - jnp.sum(pred, axis=0)
    chi = jnp.sum(resid * resid)
    xfull = split22(resid[None] + pred)
    a_one = join22(matmul22(xfull, herm(y_one)))
    a_two = join22(matmul22(herm(xfull), herm(y_two)))
    term_p = jnp.concatenate([a_one, gram_parts(y_one)], axis=1)
    term_q = jnp.concatenate([a_two, gram_parts(y_two)], axis=1)
    return term_p, term_q, chi


def accumulate(term_p, term_q, first_station, second_station, count):
    summed = jax.ops.segment_sum(jnp.moveaxis(term_p, 3, 0), first_station, num_segments=count)
    summed = summed + jax.ops.segment_sum(jnp.moveaxis(term_q, 3, 0), second_station, num_segments=count)
    return jnp.moveaxis(summed, 0, 3)


def solve(normals, gains):
    amat = split22(normals[:, :8])
    diag_one = normals[:, 8] + REG
    diag_two = normals[:, 9] + REG
    off_re = normals[:, 10]
    off_im = normals[:, 11]
    det = diag_one * diag_two - off_re * off_re - off_im * off_im
    zeros = jnp.zeros_like(det)
    inverse = [(diag_two / det, zeros), (-off_re / det, -off_im / det),
               (-off_re / det, off_im / det), (diag_one / det, zeros)]
    fresh = join22(matmul22(amat, inverse))
    return 0.5 * (gains + fresh)


def identity_like(gains):
    ident = jnp.array([1.0, 0.0, 0.0, 0.0, 0.0, 0.0, 1.0, 0.0], dtype=jnp.float32)
    return ident[None, :, None, None] + jnp.zeros_like(gains)


def reference(visibilities, model, first_station, second_station, gain_offset):
    vis_c = jnp.moveaxis(visibilities, 1, 0)[:, :, None, :]
    mod_c = jnp.moveaxis(model, 2, 0)[:, :, :, None, :]
    off_c = jnp.moveaxis(gain_offset, 2, 0)[:, :, :, None, :]

    def one_channel(inputs):
        vis_one, mod_one, off_one = inputs
        gains = identity_like(off_one) + off_one
        chis = []
        for step in range(ITERS):
            gain_p = jnp.take(gains, first_station, axis=3)
            gain_q = jnp.take(gains, second_station, axis=3)
            term_p, term_q, chi = station_terms(gain_p, gain_q, mod_one, vis_one)
            chis.append(chi)
            normals = accumulate(term_p, term_q, first_station, second_station, STATION_COUNT)
            gains = solve(normals, gains)
        return gains[:, :, 0, :], jnp.stack(chis)

    gains_c, misfit_complex = lax.map(one_channel, (vis_c, mod_c, off_c))
    gains = jnp.moveaxis(gains_c, 0, 2)
    misfit = jnp.sum(misfit_complex, axis=0) / (8.0 * BASELINE_TOTAL * CHANNEL_COUNT)
    padded = jnp.pad(gains, ((0, 0), (0, 0), (SPAN, SPAN), (0, 0)))
    chan = jnp.arange(CHANNEL_COUNT, dtype=jnp.int32)
    numer = jnp.zeros_like(gains)
    denom = jnp.zeros((CHANNEL_COUNT,), jnp.float32)
    for shift in range(-SPAN, SPAN + 1):
        weight = jnp.exp(jnp.float32(-(shift * shift) / (2.0 * KERNEL_VAR)))
        numer = numer + weight * padded[:, :, SPAN + shift:SPAN + shift + CHANNEL_COUNT, :]
        valid = ((chan + shift >= 0) & (chan + shift < CHANNEL_COUNT)).astype(jnp.float32)
        denom = denom + weight * valid
    smoothed = numer / denom[None, None, :, None]
    return smoothed, misfit
```

```python
import functools

import jax
import jax.numpy as jnp
from jax import lax
from jax.experimental import pallas as pl
from jax.experimental.pallas import tpu as pltpu
from jax.sharding import PartitionSpec as P

STATION_COUNT = 512
ITERS = 3
SPAN = 4
REG = 1.0
KERNEL_VAR = 4.0
BLOCK = 256
F32 = jnp.float32
BF16 = jnp.bfloat16


def cmul(a, b):
    return (a[0] * b[0] - a[1] * b[1], a[0] * b[1] + a[1] * b[0])


def cadd(a, b):
    return (a[0] + b[0], a[1] + b[1])


def conj(a):
    return (a[0], -a[1])


def matmul22(a, b):
    return [
        cadd(cmul(a[0], b[0]), cmul(a[1], b[2])),
        cadd(cmul(a[0], b[1]), cmul(a[1], b[3])),
        cadd(cmul(a[2], b[0]), cmul(a[3], b[2])),
        cadd(cmul(a[2], b[1]), cmul(a[3], b[3])),
    ]


def herm(a):
    return [conj(a[0]), conj(a[2]), conj(a[1]), conj(a[3])]


def gram_parts(y):
    diag_one = y[0][0] ** 2 + y[0][1] ** 2 + y[1][0] ** 2 + y[1][1] ** 2
    diag_two = y[2][0] ** 2 + y[2][1] ** 2 + y[3][0] ** 2 + y[3][1] ** 2
    off = cadd(cmul(y[0], conj(y[2])), cmul(y[1], conj(y[3])))
    return [diag_one, diag_two, off[0], off[1]]


def flat(m):
    return [m[k][j] for k in range(4) for j in range(2)]


def pairs(parts):
    return [(parts[2 * k], parts[2 * k + 1]) for k in range(4)]


def nt_dot(a, b):
    return lax.dot_general(a, b, (((1,), (1,)), ((), ())), preferred_element_type=F32)


def kernel(
    chips,
    nch,
    model_ref,
    vis_ref,
    stat_ref,
    goff_ref,
    out_ref,
    chi_ref,
    m_all,
    m_stage,
    v_all,
    s_all,
    onehot,
    gains,
    gains_hl,
    own_t,
    term_a,
    term_b,
    norm,
    recv,
    chi_acc,
    fin,
    chi_send,
    chi_recv,
    ex_send,
    ex_recv,
    rs_send,
    rs_recv,
    ag_send,
    ag_recv,
    fin_send,
    fin_recv,
    chi_ssem,
    chi_rsem,
):
    nb = vis_ref.shape[2]
    total_b = 2 * nb
    st = STATION_COUNT // chips
    half = st // 2
    rows = st + half
    me = lax.axis_index("bl")
    z = lax.axis_index("ch")
    chip = me // 2
    core = me % 2
    sib = chip * 2 + (1 - core)

    def there(bl, ch=None):
        return {"bl": bl, "ch": z if ch is None else ch}

    def peer(k):
        return (chip + k) % chips

    def send(src, dst, ssem, rsem, where):
        return pltpu.make_async_remote_copy(
            src_ref=src, dst_ref=dst, send_sem=ssem, recv_sem=rsem,
            device_id=where, device_id_type=pl.DeviceIdType.MESH)

    barrier = pltpu.get_barrier_semaphore()

    def greet_bl(k, carry):
        pl.semaphore_signal(barrier, inc=1, device_id=there(peer(k) * 2 + core),
                            device_id_type=pl.DeviceIdType.MESH)
        return carry

    def greet_ch(k, carry):
        pl.semaphore_signal(
            barrier, inc=1,
            device_id=there(chip * 2 + (core + k) % 2, (z + k // 2) % nch),
            device_id_type=pl.DeviceIdType.MESH)
        return carry

    lax.fori_loop(1, 2 * nch, greet_ch, 0)
    lax.fori_loop(1, chips, greet_bl, 0)

    r = lax.broadcasted_iota(jnp.int32, (256, 256), 0)
    q = lax.broadcasted_iota(jnp.int32, (256, 256), 1)
    h = lax.shift_right_logical(r, 7)
    c_two = lax.shift_right_logical(r, 6) & 1
    comp = lax.shift_right_logical(r, 3) & 7
    direction = r & 7
    chan = 2 * ((core + h) & 1) + c_two
    perm = jnp.where(q == direction * 32 + comp * 4 + chan, 1.0, 0.0).astype(BF16)
    permuted = jnp.dot(perm, model_ref[...], preferred_element_type=F32)
    m_all[:, :nb] = permuted[:128]
    m_stage[...] = permuted[128:]
    v_all[:, :nb] = vis_ref[0]
    s_all[:, :nb] = stat_ref[...]
    own_rows = pl.ds(pl.multiple_of(me * half, half), half)
    gains[own_rows, :] = goff_ref[0]

    pl.semaphore_wait(barrier, 2 * nch - 1 + chips - 1)

    swaps = [
        send(goff_ref.at[1], gains.at[own_rows, :], ex_send.at[0], ex_recv.at[0], there(sib)),
        send(stat_ref, s_all.at[:, pl.ds(nb, nb)], ex_send.at[1], ex_recv.at[1], there(sib)),
        send(m_stage, m_all.at[:, pl.ds(nb, nb)], ex_send.at[2], ex_recv.at[2], there(sib)),
        send(vis_ref.at[1], v_all.at[:, pl.ds(nb, nb)], ex_send.at[3], ex_recv.at[3], there(sib)),
    ]
    for swap in swaps:
        swap.start()
    chip_rows = pl.ds(pl.multiple_of(chip * st, st), st)

    def ag_copy(k):
        return send(gains.at[chip_rows, :], gains.at[chip_rows, :],
                    ag_send.at[k - 1], ag_recv.at[k - 1], there(peer(k) * 2 + core))

    def ag_start(k, carry):
        ag_copy(k).start()
        return carry

    def ag_wait_recv(k, carry):
        ag_copy(k).wait_recv()
        return carry

    def ag_wait_send(k, carry):
        ag_copy(k).wait_send()
        return carry

    swaps[0].wait_recv()
    lax.fori_loop(1, chips, ag_start, 0)
    own_t[...] = jnp.transpose(gains[chip_rows, :])

    station = lax.broadcasted_iota(jnp.int32, (STATION_COUNT, BLOCK), 0)

    def hot(i, carry):
        at = pl.multiple_of(i * BLOCK, BLOCK)
        for j in range(2):
            which = s_all[j:j + 1, pl.ds(at, BLOCK)]
            onehot[:, pl.ds(pl.multiple_of(j * total_b + at, BLOCK), BLOCK)] = jnp.where(
                station == which, 1.0, 0.0).astype(BF16)
        return carry

    lax.fori_loop(0, nb // BLOCK, hot, 0)
    swaps[1].wait_recv()
    lax.fori_loop(nb // BLOCK, total_b // BLOCK, hot, 0)
    swaps[2].wait_recv()
    swaps[3].wait_recv()
    for swap in swaps:
        swap.wait_send()
    chi_acc[...] = jnp.zeros_like(chi_acc)
    lax.fori_loop(1, chips, ag_wait_recv, 0)
    lax.fori_loop(1, chips, ag_wait_send, 0)

    def store_pair(ref, at_row, lo_row, cols, one, two, dup):
        both = jnp.concatenate([one, two], axis=0)
        hi = both.astype(BF16)
        lo = (both - hi.astype(F32)).astype(BF16)
        ref[at_row:at_row + 16, cols] = hi
        ref[lo_row:lo_row + 16, cols] = lo
        if dup:
            ref[at_row + dup:at_row + dup + 16, cols] = hi
            ref[lo_row + dup:lo_row + dup + 16, cols] = lo

    def terms(step):
        def body(i, carry):
            at = pl.multiple_of(i * BLOCK, BLOCK)
            cols = pl.ds(at, BLOCK)
            cols_q = pl.ds(pl.multiple_of(total_b + at, BLOCK), BLOCK)
            both = gains_hl[...]
            gp = jnp.dot(both, onehot[:, cols], preferred_element_type=F32)
            gp = gp[:128] + gp[128:]
            gq = jnp.dot(both, onehot[:, cols_q], preferred_element_type=F32)
            gq = gq[:128] + gq[128:]
            chi = jnp.zeros((1, BLOCK), F32)
            for c in range(2):
                def part(x):
                    return pairs([x[c * 64 + 8 * k:c * 64 + 8 * k + 8] for k in range(8)])

                jp = part(gp)
                jq = part(gq)
                mod = pairs([m_all[c * 64 + 8 * k:c * 64 + 8 * k + 8, cols] for k in range(8)])
                y_one = matmul22(mod, herm(jq))
                pred = flat(matmul22(jp, y_one))
                y_two = matmul22(herm(mod), herm(jp))
                resid = []
                for k in range(8):
                    one = v_all[c * 8 + k:c * 8 + k + 1, cols] - jnp.sum(pred[k], axis=0, keepdims=True)
                    chi = chi + one * one
                    resid.append(one)
                resid = pairs(resid)
                a_one = flat(matmul22(resid, herm(y_one)))
                a_two = flat(matmul22(herm(resid), herm(y_two)))
                b_one = gram_parts(y_one)
                b_two = gram_parts(y_two)
                for k in range(0, 8, 2):
                    row = c * 64 + 8 * k
                    store_pair(term_a, row, 128 + row, cols, a_one[k], a_one[k + 1], 0)
                    store_pair(term_a, row, 128 + row, cols_q, a_two[k], a_two[k + 1], 0)
                for k in range(0, 4, 2):
                    row = c * 32 + 8 * k
                    store_pair(term_b, row, 128 + row, cols, b_one[k], b_one[k + 1], 64)
                    store_pair(term_b, row, 128 + row, cols_q, b_two[k], b_two[k + 1], 64)
            sums = chi[:, :128]
            for j in range(128, BLOCK, 128):
                sums = sums + chi[:, j:j + 128]
            chi_acc[pl.ds(step, 1), :] += sums
            return carry

        lax.fori_loop(0, total_b // BLOCK, body, 0)

    lane = lax.broadcasted_iota(jnp.int32, (half, 128), 1)

    def iteration(step, last):
        size = rows + 8 if last else rows
        turned = jnp.transpose(gains[...])
        hi = turned.astype(BF16)
        gains_hl[:128] = hi
        gains_hl[128:] = (turned - hi.astype(F32)).astype(BF16)
        terms(step)
        group = max(st, 256)

        for g in range(STATION_COUNT // group):
            hot_rows = onehot[g * group:(g + 1) * group, :]
            na = nt_dot(hot_rows, term_a[...])
            na = na[:, :128] + na[:, 128:]
            nb_ = nt_dot(hot_rows, term_b[...])
            nb_ = nb_[:, :128] + nb_[:, 128:]
            for j in range(group // st):
                chunk = g * (group // st) + j
                norm[chunk, :st, :] = na[j * st:(j + 1) * st]
                norm[chunk, st:rows, :] = jnp.where(
                    lane < 64, nb_[j * st:j * st + half], nb_[j * st + half:(j + 1) * st])
                if last:
                    norm[chunk, rows:rows + 8, :] = chi_acc[...]

        def rs_copy(k):
            return send(norm.at[peer(k), pl.ds(0, size), :],
                        recv.at[k - 1, pl.ds(0, size), :],
                        rs_send.at[k - 1], rs_recv.at[k - 1], there(peer(k) * 2 + core))

        def rs_start(k, carry):
            rs_copy(k).start()
            return carry

        lax.fori_loop(1, chips, rs_start, 0)

        def rs_take(k, total):
            rs_copy(k).wait_recv()
            return total + recv[k - 1, :size, :]

        total = lax.fori_loop(1, chips, rs_take, norm[chip, :size, :])

        def rs_wait_send(k, carry):
            rs_copy(k).wait_send()
            return carry

        r_t = jnp.transpose(total[:st])
        packed = total[st:rows]
        unpacked = jnp.concatenate([packed, pltpu.roll(packed, 64, 1)], axis=0)
        b_t = jnp.transpose(unpacked)
        fresh_rows = []
        for c in range(2):
            old = [own_t[c * 64 + 8 * k:c * 64 + 8 * k + 8, :] for k in range(8)]
            amat = pairs([r_t[c * 64 + 8 * k:c * 64 + 8 * k + 8, :] - old[k] for k in range(8)])
            diag_one, diag_two, off_re, off_im = [
                b_t[c * 32 + 8 * k:c * 32 + 8 * k + 8, :] for k in range(4)]
            diag_one = diag_one + REG
            diag_two = diag_two + REG
            det = diag_one * diag_two - off_re * off_re - off_im * off_im
            scale = 0.5 / det
            d_one = diag_one * scale
            d_two = diag_two * scale
            o_re = off_re * scale
            o_im = off_im * scale
            for row in range(2):
                a0 = amat[2 * row]
                a1 = amat[2 * row + 1]
                n0 = cadd((a0[0] * d_two, a0[1] * d_two), cmul(a1, (-o_re, o_im)))
                n1 = cadd(cmul(a0, (-o_re, -o_im)), (a1[0] * d_one, a1[1] * d_one))
                k = 4 * row
                fresh_rows += [old[k] + n0[0], old[k + 1] + n0[1],
                               old[k + 2] + n1[0], old[k + 3] + n1[1]]
        fresh = jnp.concatenate(fresh_rows, axis=0)
        own_t[...] = fresh
        gains[chip_rows, :] = jnp.transpose(fresh)
        if not last:
            lax.fori_loop(1, chips, ag_start, 0)
        lax.fori_loop(1, chips, rs_wait_send, 0)
        if not last:
            lax.fori_loop(1, chips, ag_wait_recv, 0)
            lax.fori_loop(1, chips, ag_wait_send, 0)
        return total[rows:] if last else None

    def early(step, carry):
        iteration(step, False)
        return carry

    lax.fori_loop(0, ITERS - 1, early, 0)
    chi_total = iteration(ITERS - 1, True)

    chi_send[...] = chi_total
    base = chip * st

    def half_rows(which):
        return pl.ds(pl.multiple_of(base + which * half, half), half)

    def chi_copy(k):
        return send(chi_send, chi_recv.at[k - 1], chi_ssem.at[k - 1], chi_rsem.at[k - 1],
                    there(chip * 2 + (core + k) % 2, (z + k // 2) % nch))

    def up(which):
        return send(gains.at[half_rows(which), :], fin.at[0, core], fin_send.at[which],
                    fin_recv.at[0, core], there(chip * 2 + which, (z + 1) % nch))

    def down(which):
        return send(gains.at[half_rows(which), :], fin.at[2, core], fin_send.at[2 + which],
                    fin_recv.at[2, core], there(chip * 2 + which, (z + nch - 1) % nch))

    across = send(gains.at[half_rows(1 - core), :], fin.at[1, core], fin_send.at[4],
                  fin_recv.at[1, core], there(sib))

    across.start()

    @pl.when(z < nch - 1)
    def _():
        for which in range(2):
            up(which).start()

    @pl.when(z > 0)
    def _():
        for which in range(2):
            down(which).start()

    def chi_start(k, carry):
        chi_copy(k).start()
        return carry

    lax.fori_loop(1, 2 * nch, chi_start, 0)
    fin[1, core] = gains[half_rows(core), :]

    def wait_fin(slot, source):
        send(fin.at[slot, source], fin.at[slot, source], fin_send.at[0],
             fin_recv.at[slot, source], there(sib)).wait_recv()

    @pl.when(z > 0)
    def _():
        for source in range(2):
            wait_fin(0, source)

    @pl.when(z == 0)
    def _():
        fin[0] = jnp.zeros(fin.shape[1:], F32)

    @pl.when(z < nch - 1)
    def _():
        for source in range(2):
            wait_fin(2, source)

    @pl.when(z == nch - 1)
    def _():
        fin[2] = jnp.zeros(fin.shape[1:], F32)

    wait_fin(1, 1 - core)

    slabs = []
    for slot in range(3):
        for source in range(2):
            turned = jnp.transpose(fin[slot, source])
            slabs += [turned[:64], turned[64:]]
    weights = [jnp.exp(jnp.full((1, 1), -(s * s) / (2.0 * KERNEL_VAR), F32)) for s in range(-SPAN, SPAN + 1)]
    for c in range(4):
        numer = jnp.zeros_like(slabs[0])
        denom = jnp.zeros((1, 1), F32)
        for s in range(-SPAN, SPAN + 1):
            weight = weights[s + SPAN]
            numer = numer + weight * slabs[4 + c + s]
            at = z * 4 + c + s
            valid = jnp.where((at >= 0) & (at < 4 * nch), 1.0, 0.0).astype(F32)
            denom = denom + weight * valid
        out_ref[c] = numer / denom

    def chi_take(k, total):
        chi_copy(k).wait_recv()
        return total + chi_recv[k - 1]

    chi_all = lax.fori_loop(1, 2 * nch, chi_take, chi_total)
    chi_ref[...] = jnp.broadcast_to(jnp.sum(chi_all, axis=1, keepdims=True), (8, 128))

    def chi_wait_send(k, carry):
        chi_copy(k).wait_send()
        return carry

    lax.fori_loop(1, 2 * nch, chi_wait_send, 0)
    across.wait_send()

    @pl.when(z < nch - 1)
    def _():
        for which in range(2):
            up(which).wait_send()

    @pl.when(z > 0)
    def _():
        for which in range(2):
            down(which).wait_send()


def on_device(visibilities, model, first_station, second_station, gain_offset):
    nb = visibilities.shape[2]
    half = gain_offset.shape[3]
    st = 2 * half
    chips = lax.axis_size("bl") // 2
    nch = lax.axis_size("ch")
    rows = st + half
    total_b = 2 * nb
    core = lax.axis_index("bl") % 2
    mine = core == 0

    model2d = model.reshape(256, nb)
    vis = jnp.transpose(visibilities, (1, 0, 2)).reshape(2, 16, nb)
    vis = jnp.where(mine, vis, vis[::-1])
    stat = jnp.concatenate([first_station[None], second_station[None], jnp.zeros((6, nb), jnp.int32)], axis=0)
    ident = jnp.array([1.0, 0.0, 0.0, 0.0, 0.0, 0.0, 1.0, 0.0], dtype=F32)
    goff = ident[None, :, None, None] + gain_offset
    goff = jnp.transpose(goff, (2, 3, 1, 0)).reshape(2, 2, half, 64)
    goff = jnp.transpose(goff, (0, 2, 1, 3)).reshape(2, half, 128)
    goff = jnp.where(mine, goff, goff[::-1])

    vmem = pl.BlockSpec(memory_space=pltpu.VMEM)
    dma = pltpu.SemaphoreType.DMA
    smooth, chi = pl.pallas_call(
        functools.partial(kernel, chips, nch),
        out_shape=(
            jax.ShapeDtypeStruct((4, 64, half), F32),
            jax.ShapeDtypeStruct((8, 128), F32),
        ),
        in_specs=[vmem] * 4,
        out_specs=(vmem, vmem),
        scratch_shapes=[
            pltpu.VMEM((128, total_b), F32),
            pltpu.VMEM((128, nb), F32),
            pltpu.VMEM((16, total_b), F32),
            pltpu.VMEM((8, total_b), jnp.int32),
            pltpu.VMEM((STATION_COUNT, 2 * total_b), BF16),
            pltpu.VMEM((STATION_COUNT, 128), F32),
            pltpu.VMEM((256, STATION_COUNT), BF16),
            pltpu.VMEM((128, st), F32),
            pltpu.VMEM((256, 2 * total_b), BF16),
            pltpu.VMEM((256, 2 * total_b), BF16),
            pltpu.VMEM((chips, rows + 8, 128), F32),
            pltpu.VMEM((chips - 1, rows + 8, 128), F32),
            pltpu.VMEM((8, 128), F32),
            pltpu.VMEM((3, 2, half, 128), F32),
            pltpu.VMEM((8, 128), F32),
            pltpu.VMEM((2 * nch - 1, 8, 128), F32),
            dma((4,)),
            dma((4,)),
            dma((chips - 1,)),
            dma((chips - 1,)),
            dma((chips - 1,)),
            dma((chips - 1,)),
            dma((5,)),
            dma((3, 2)),
            dma((2 * nch - 1,)),
            dma((2 * nch - 1,)),
        ],
        compiler_params=pltpu.CompilerParams(
            collective_id=0, has_side_effects=True, vmem_limit_bytes=48 * 1024 * 1024),
    )(model2d, vis, stat, goff)
    smoothed = jnp.transpose(smooth.reshape(4, 8, 8, half), (2, 1, 0, 3))
    count_vis = 8.0 * nb * lax.axis_size("bl") * 4 * nch
    misfit = chi[:ITERS, 0] / count_vis
    return (smoothed, misfit)


def solution(mesh):
    return jax.shard_map(
        on_device,
        mesh=mesh,
        in_specs=(
            P(None, "ch", "bl"),
            P(None, None, "ch", "bl"),
            P("bl"),
            P("bl"),
            P(None, None, "ch", "bl"),
        ),
        out_specs=(P(None, None, "ch", "bl"), P()),
        check_vma=False,
    )
```

```python
import functools

import jax
import jax.numpy as jnp
from jax import lax
from jax.experimental import pallas as pl
from jax.experimental.pallas import tpu as pltpu
from jax.sharding import PartitionSpec as P

STATION_COUNT = 512
ITERS = 3
SPAN = 4
REG = 1.0
KERNEL_VAR = 4.0
BLOCK = 256
F32 = jnp.float32
BF16 = jnp.bfloat16


def cmul(a, b):
    return (a[0] * b[0] - a[1] * b[1], a[0] * b[1] + a[1] * b[0])


def cadd(a, b):
    return (a[0] + b[0], a[1] + b[1])


def conj(a):
    return (a[0], -a[1])


def matmul22(a, b):
    return [
        cadd(cmul(a[0], b[0]), cmul(a[1], b[2])),
        cadd(cmul(a[0], b[1]), cmul(a[1], b[3])),
        cadd(cmul(a[2], b[0]), cmul(a[3], b[2])),
        cadd(cmul(a[2], b[1]), cmul(a[3], b[3])),
    ]


def herm(a):
    return [conj(a[0]), conj(a[2]), conj(a[1]), conj(a[3])]


def gram_parts(y):
    diag_one = y[0][0] ** 2 + y[0][1] ** 2 + y[1][0] ** 2 + y[1][1] ** 2
    diag_two = y[2][0] ** 2 + y[2][1] ** 2 + y[3][0] ** 2 + y[3][1] ** 2
    off = cadd(cmul(y[0], conj(y[2])), cmul(y[1], conj(y[3])))
    return [diag_one, diag_two, off[0], off[1]]


def flat(m):
    return [m[k][j] for k in range(4) for j in range(2)]


def pairs(parts):
    return [(parts[2 * k], parts[2 * k + 1]) for k in range(4)]


def nt_dot(a, b):
    return lax.dot_general(a, b, (((1,), (1,)), ((), ())), preferred_element_type=F32)


def plane(chips):
    ny = 1
    while ny * ny < chips:
        ny *= 2
    return (chips // ny, ny)


def far_first(chips):
    nx, ny = plane(chips)

    def hops(o):
        return min(o[0], nx - o[0]) + min(o[1], ny - o[1])

    others = [(i, j) for i in range(nx) for j in range(ny) if i + j > 0]
    return sorted(others, key=lambda o: -hops(o))


def kernel(
    chips,
    nch,
    vis_hbm,
    model_hbm,
    first_hbm,
    second_hbm,
    goff_hbm,
    out_ref,
    chi_ref,
    vis_in,
    model_in,
    first_in,
    second_in,
    goff_in,
    m_all,
    m_stage,
    v_all,
    v_stage,
    s_all,
    g_stage,
    onehot,
    gains,
    gains_hl,
    own_t,
    term,
    norm,
    recv,
    chi_acc,
    chi_plane,
    chi_xy,
    chi_z,
    fin,
    in_sem,
    ex_send,
    ex_recv,
    rs_send,
    rs_recv,
    ag_send,
    ag_recv,
    fin_send,
    fin_recv,
    xy_send,
    xy_recv,
    z_send,
    z_recv,
):
    nb = vis_in.shape[2]
    total_b = 2 * nb
    half = goff_in.shape[3]
    quarter = half // 2
    side = chips * half
    size = half + quarter
    nx, ny = plane(chips)
    offsets = far_first(chips)
    peers = len(offsets)
    me = lax.axis_index("bl")
    z = lax.axis_index("ch")
    chip = me // 2
    core = me % 2
    sib = chip * 2 + (1 - core)
    px = chip // ny
    py = chip % ny
    lanes = 128

    def there(bl, ch=None):
        return {"bl": bl, "ch": z if ch is None else ch}

    def peer(k):
        return ((px + offsets[k][0]) % nx) * ny + (py + offsets[k][1]) % ny

    def send(src, dst, ssem, rsem, where):
        return pltpu.make_async_remote_copy(
            src_ref=src, dst_ref=dst, send_sem=ssem, recv_sem=rsem,
            device_id=where, device_id_type=pl.DeviceIdType.MESH)

    def along_z(k):
        return there(chip * 2 + (core + k) % 2, (z + k // 2) % nch)

    z_order = sorted(range(1, 2 * nch), key=lambda k: -min(k // 2, nch - k // 2))

    barrier = pltpu.get_barrier_semaphore()
    for k in z_order:
        pl.semaphore_signal(barrier, inc=1, device_id=along_z(k),
                            device_id_type=pl.DeviceIdType.MESH)
    for k in range(peers):
        pl.semaphore_signal(barrier, inc=1, device_id=there(peer(k) * 2 + core),
                            device_id_type=pl.DeviceIdType.MESH)

    loads = [
        pltpu.make_async_copy(goff_hbm, goff_in, in_sem.at[0]),
        pltpu.make_async_copy(model_hbm, model_in, in_sem.at[1]),
        pltpu.make_async_copy(vis_hbm, vis_in, in_sem.at[2]),
        pltpu.make_async_copy(first_hbm, first_in, in_sem.at[3]),
        pltpu.make_async_copy(second_hbm, second_in, in_sem.at[4]),
    ]
    for load in loads:
        load.start()

    r = lax.broadcasted_iota(jnp.int32, (256, 256), 0)
    q = lax.broadcasted_iota(jnp.int32, (256, 256), 1)
    chan = 2 * ((core + r // 128) & 1) + (r // 64) % 2
    perm = jnp.where(q == (r % 8) * 32 + ((r // 8) % 8) * 4 + chan, 1.0, 0.0).astype(BF16)

    loads[0].wait()
    offs = goff_in[...].reshape(256, half)
    hi = offs.astype(BF16)
    rest = offs - hi.astype(F32)
    mid = rest.astype(BF16)
    low = (rest - mid.astype(F32)).astype(BF16)
    turned = [jnp.dot(perm, one, preferred_element_type=F32) for one in (hi, mid, low)]
    comp = (lax.broadcasted_iota(jnp.int32, (256, half), 0) // 8) % 8
    start = jnp.where((comp == 0) | (comp == 6), 1.0, 0.0) + ((turned[0] + turned[1]) + turned[2])
    here_rows = pl.ds(pl.multiple_of(core * 64, 64), 64)
    for c in range(2):
        own_t[c, here_rows, :] = start[c * 64:c * 64 + 64]
        g_stage[c] = start[128 + c * 64:192 + c * 64]

    loads[1].wait()
    permuted = jnp.dot(perm, model_in[...].reshape(256, nb), preferred_element_type=F32)
    m_all[:, :nb] = permuted[:128]
    m_stage[...] = permuted[128:]
    loads[2].wait()
    for c in range(2):
        for k in range(8):
            row = c * 8 + k
            v_all[row:row + 1, :nb] = vis_in[k, pl.ds(2 * core + c, 1), :]
            v_stage[row:row + 1, :] = vis_in[k, pl.ds(2 * (1 - core) + c, 1), :]
    loads[3].wait()
    loads[4].wait()

    def place(s):
        rem = s % (2 * half)
        return (rem // half) * side + (s // (2 * half)) * half + rem % half

    s_all[0, 0:1, :] = place(first_in[...])
    s_all[0, 1:2, :] = place(second_in[...])
    s_all[0, 2:8, :] = jnp.zeros((6, nb), jnp.int32)

    station = lax.broadcasted_iota(jnp.int32, (STATION_COUNT, BLOCK), 0)

    def hot(part):
        def body(i, carry):
            at = pl.multiple_of(i * BLOCK, BLOCK)
            for j in range(2):
                which = s_all[part, j:j + 1, pl.ds(at, BLOCK)]
                to = pl.multiple_of(j * total_b + part * nb + at, BLOCK)
                onehot[:, pl.ds(to, BLOCK)] = jnp.where(station == which, 1.0, 0.0).astype(BF16)
            return carry

        lax.fori_loop(0, nb // BLOCK, body, 0)

    chi_acc[...] = jnp.zeros_like(chi_acc)
    pl.semaphore_wait(barrier, 2 * nch - 1 + peers)

    swaps = [
        send(g_stage, own_t.at[:, here_rows, :], ex_send.at[0], ex_recv.at[0], there(sib)),
        send(s_all.at[0], s_all.at[1], ex_send.at[1], ex_recv.at[1], there(sib)),
        send(m_stage, m_all.at[:, pl.ds(nb, nb)], ex_send.at[2], ex_recv.at[2], there(sib)),
        send(v_stage, v_all.at[:, pl.ds(nb, nb)], ex_send.at[3], ex_recv.at[3], there(sib)),
    ]
    for swap in swaps:
        swap.start()
    chip_rows = pl.ds(pl.multiple_of(chip * half, half), half)

    def ag_copy(c, k):
        return send(gains.at[c, chip_rows, :], gains.at[c, chip_rows, :],
                    ag_send.at[c, k], ag_recv.at[c, k], there(peer(k) * 2 + core))

    swaps[0].wait_recv()
    for c in range(2):
        gains[c, chip_rows, :] = jnp.transpose(own_t[c])
        for k in range(peers):
            ag_copy(c, k).start()
    hot(0)
    swaps[1].wait_recv()
    hot(1)
    swaps[2].wait_recv()
    swaps[3].wait_recv()
    for swap in swaps:
        swap.wait_send()

    def store_pair(c, row, cols, one, two):
        both = jnp.concatenate([one, two], axis=0)
        hi = both.astype(BF16)
        term[c, row:row + 16, cols] = hi
        term[c, 128 + row:144 + row, cols] = (both - hi.astype(F32)).astype(BF16)

    def terms(c, step):
        both = gains_hl[c]
        chi = jnp.zeros((1, lanes), F32)
        for i in range(total_b // BLOCK):
            cols = pl.ds(i * BLOCK, BLOCK)
            cols_q = pl.ds(total_b + i * BLOCK, BLOCK)
            gp = jnp.dot(both, onehot[:, cols], preferred_element_type=F32)
            gp = gp[:64] + gp[64:]
            gq = jnp.dot(both, onehot[:, cols_q], preferred_element_type=F32)
            gq = gq[:64] + gq[64:]

            def part(x):
                return pairs([x[8 * k:8 * k + 8] for k in range(8)])

            jp = part(gp)
            jq = part(gq)
            mod = pairs([m_all[c * 64 + 8 * k:c * 64 + 8 * k + 8, cols] for k in range(8)])
            y_one = matmul22(mod, herm(jq))
            pred = flat(matmul22(jp, y_one))
            y_two = matmul22(herm(mod), herm(jp))
            resid = []
            for k in range(8):
                one = v_all[c * 8 + k:c * 8 + k + 1, cols] - jnp.sum(pred[k], axis=0, keepdims=True)
                for j in range(0, BLOCK, lanes):
                    chi = chi + one[:, j:j + lanes] * one[:, j:j + lanes]
                resid.append(one)
            resid = pairs(resid)
            a_one = flat(matmul22(resid, herm(y_one))) + gram_parts(y_one)
            a_two = flat(matmul22(herm(resid), herm(y_two))) + gram_parts(y_two)
            for k in range(0, 12, 2):
                store_pair(c, 8 * k, cols, a_one[k], a_one[k + 1])
                store_pair(c, 8 * k, cols_q, a_two[k], a_two[k + 1])
        chi_acc[pl.ds(step, 1), :] += chi

    lane_a = lax.broadcasted_iota(jnp.int32, (side, lanes), 1)
    lane_b = lax.broadcasted_iota(jnp.int32, (quarter, lanes), 1)

    def rs_copy(c, k):
        return send(norm.at[c, peer(k)], recv.at[c, k], rs_send.at[c, k], rs_recv.at[c, k],
                    there(peer(k) * 2 + core))

    def scatter(c):
        sums = nt_dot(onehot[...], term[c])
        sums = sums[:, :lanes] + sums[:, lanes:]
        lower = sums[:side]
        upper = pltpu.roll(sums[side:], 64, 1)
        packed = jnp.where(lane_a < 64, lower, upper)
        for j in range(chips):
            norm[c, j, :half, :] = packed[j * half:(j + 1) * half]
            mid_row = j * half + quarter
            end = (j + 1) * half
            low_one = lower[j * half:mid_row]
            low_two = pltpu.roll(lower[mid_row:end], 32, 1)
            up_one = upper[j * half:mid_row]
            up_two = pltpu.roll(upper[mid_row:end], 32, 1)
            norm[c, j, half:size, :] = jnp.where(
                lane_b < 64,
                jnp.where(lane_b < 32, up_one, up_two),
                jnp.where(lane_b < 96, low_one, low_two))
        for k in range(peers):
            rs_copy(c, k).start()

    def solve(c):
        total = norm[c, chip]
        for k in reversed(range(peers)):
            rs_copy(c, k).wait_recv()
            total = total + recv[c, k]
        r_t = jnp.transpose(total[:half])
        b_t = jnp.transpose(jnp.concatenate(
            [total[half:], pltpu.roll(total[half:], 96, 1)], axis=0))
        fresh_rows = []
        for h in range(2):
            old = [own_t[c, h * 64 + 8 * k:h * 64 + 8 * k + 8, :] for k in range(8)]
            amat = pairs([r_t[h * 64 + 8 * k:h * 64 + 8 * k + 8, :] - old[k] for k in range(8)])
            base = 64 * (1 - h)
            diag_one, diag_two, off_re, off_im = [
                b_t[base + 8 * k:base + 8 * k + 8, :] for k in range(4)]
            diag_one = diag_one + REG
            diag_two = diag_two + REG
            det = diag_one * diag_two - off_re * off_re - off_im * off_im
            scale = 0.5 / det
            d_one = diag_one * scale
            d_two = diag_two * scale
            o_re = off_re * scale
            o_im = off_im * scale
            for row in range(2):
                a0 = amat[2 * row]
                a1 = amat[2 * row + 1]
                n0 = cadd((a0[0] * d_two, a0[1] * d_two), cmul(a1, (-o_re, o_im)))
                n1 = cadd(cmul(a0, (-o_re, -o_im)), (a1[0] * d_one, a1[1] * d_one))
                k = 4 * row
                fresh_rows += [old[k] + n0[0], old[k + 1] + n0[1],
                               old[k + 2] + n1[0], old[k + 3] + n1[1]]
        fresh = jnp.concatenate(fresh_rows, axis=0)
        own_t[c] = fresh
        return jnp.transpose(fresh)

    def prepare(c):
        for k in reversed(range(peers)):
            ag_copy(c, k).wait_recv()
        turned = jnp.transpose(gains[c])
        turned = jnp.concatenate([turned[:64], turned[64:]], axis=1)
        hi = turned.astype(BF16)
        gains_hl[c, :64] = hi
        gains_hl[c, 64:] = (turned - hi.astype(F32)).astype(BF16)

    def after_scatter(c):
        for k in range(peers):
            ag_copy(c, k).wait_send()

    def after_solve(c):
        for k in range(peers):
            rs_copy(c, k).wait_send()

    def early(step, carry):
        for c in range(2):
            prepare(c)
            terms(c, step)
            scatter(c)
            after_scatter(c)
        for c in range(2):
            gains[c, chip_rows, :] = solve(c)
            for k in range(peers):
                ag_copy(c, k).start()
            after_solve(c)
        return carry

    lax.fori_loop(0, ITERS - 1, early, 0)

    def xy_copy(k):
        return send(chi_acc, chi_xy.at[k], xy_send.at[k], xy_recv.at[k],
                    there(peer(k) * 2 + core))

    def z_copy(k):
        return send(chi_plane, chi_z.at[k - 1], z_send.at[k - 1], z_recv.at[k - 1], along_z(k))

    def up(c, which):
        return send(fin.at[1, core, c], fin.at[0, core, c], fin_send.at[c, which],
                    fin_recv.at[0, core, c], there(chip * 2 + which, (z + 1) % nch))

    def down(c, which):
        return send(fin.at[1, core, c], fin.at[2, core, c], fin_send.at[c, 2 + which],
                    fin_recv.at[2, core, c], there(chip * 2 + which, (z + nch - 1) % nch))

    def across(c):
        return send(fin.at[1, core, c], fin.at[1, core, c], fin_send.at[c, 4],
                    fin_recv.at[1, core, c], there(sib))

    def halo(c):
        fin[1, core, c] = solve(c)

        @pl.when(z < nch - 1)
        def _():
            for which in range(2):
                up(c, which).start()

        @pl.when(z > 0)
        def _():
            for which in range(2):
                down(c, which).start()

        across(c).start()

    for c in range(2):
        prepare(c)
        terms(c, ITERS - 1)
        if c == 1:
            for k in range(peers):
                xy_copy(k).start()
        scatter(c)
        after_scatter(c)

    @pl.when(z == 0)
    def _():
        fin[0] = jnp.zeros(fin.shape[1:], F32)

    @pl.when(z == nch - 1)
    def _():
        fin[2] = jnp.zeros(fin.shape[1:], F32)

    shape = (12 * half, 4 * lanes)
    row = lax.broadcasted_iota(jnp.int32, shape, 0)
    col = lax.broadcasted_iota(jnp.int32, shape, 1)
    to = col // lanes
    shift = row // half - 4 - to

    def weigh(step):
        step = step.astype(F32)
        return jnp.exp(-(step * step) / (2.0 * KERNEL_VAR))

    line = lax.broadcasted_iota(jnp.int32, (1, 4 * lanes), 1) // lanes
    denom = jnp.zeros((1, 4 * lanes), F32)
    for s in range(-SPAN, SPAN + 1):
        at = z * 4 + line + s
        denom = denom + jnp.where((at >= 0) & (at < 4 * nch), weigh(jnp.full((1, 4 * lanes), s, jnp.int32)), 0.0)
    mixing = jnp.where(
        (row % half == col % lanes) & (shift >= -SPAN) & (shift <= SPAN), weigh(shift) / denom, 0.0)

    halo(0)
    chi = chi_acc[...]
    for k in reversed(range(peers)):
        xy_copy(k).wait_recv()
        chi = chi + chi_xy[k]
    chi_plane[...] = chi
    for k in z_order:
        z_copy(k).start()
    halo(1)
    for c in range(2):
        after_solve(c)

    def wait_fin(slot, source):
        for c in range(2):
            send(fin.at[slot, source, c], fin.at[slot, source, c], fin_send.at[c, 0],
                 fin_recv.at[slot, source, c], there(sib)).wait_recv()

    wait_fin(1, 1 - core)

    @pl.when(z > 0)
    def _():
        for source in range(2):
            wait_fin(0, source)

    @pl.when(z < nch - 1)
    def _():
        for source in range(2):
            wait_fin(2, source)

    slabs = jnp.transpose(fin[...].reshape(12 * half, lanes))
    slabs = jnp.where(core == 0, slabs[:64], slabs[64:])
    smooth = jnp.dot(slabs, mixing, precision=lax.Precision.HIGHEST, preferred_element_type=F32)
    for c in range(4):
        out_ref[c] = smooth[:, c * lanes:c * lanes + half]

    chi = chi_plane[...]
    for k in reversed(z_order):
        z_copy(k).wait_recv()
        chi = chi + chi_z[k - 1]
    chi_ref[...] = jnp.broadcast_to(jnp.sum(chi, axis=1, keepdims=True), (8, lanes))

    for k in range(peers):
        xy_copy(k).wait_send()
    for k in z_order:
        z_copy(k).wait_send()
    for c in range(2):
        across(c).wait_send()

    @pl.when(z < nch - 1)
    def _():
        for c in range(2):
            for which in range(2):
                up(c, which).wait_send()

    @pl.when(z > 0)
    def _():
        for c in range(2):
            for which in range(2):
                down(c, which).wait_send()


def on_device(visibilities, model, first_station, second_station, gain_offset):
    nb = visibilities.shape[2]
    half = gain_offset.shape[3]
    chips = lax.axis_size("bl") // 2
    nch = lax.axis_size("ch")
    size = half + half // 2
    total_b = 2 * nb
    peers = chips - 1
    vmem = pl.BlockSpec(memory_space=pltpu.VMEM)
    hbm = pl.BlockSpec(memory_space=pltpu.HBM)
    dma = pltpu.SemaphoreType.DMA
    smooth, chi = pl.pallas_call(
        functools.partial(kernel, chips, nch),
        out_shape=(
            jax.ShapeDtypeStruct((4, 64, half), F32),
            jax.ShapeDtypeStruct((8, 128), F32),
        ),
        in_specs=[hbm] * 5,
        out_specs=(vmem, vmem),
        scratch_shapes=[
            pltpu.VMEM(visibilities.shape, F32),
            pltpu.VMEM(model.shape, BF16),
            pltpu.VMEM((1, nb), jnp.int32),
            pltpu.VMEM((1, nb), jnp.int32),
            pltpu.VMEM(gain_offset.shape, F32),
            pltpu.VMEM((128, total_b), F32),
            pltpu.VMEM((128, nb), F32),
            pltpu.VMEM((16, total_b), F32),
            pltpu.VMEM((16, nb), F32),
            pltpu.VMEM((2, 8, nb), jnp.int32),
            pltpu.VMEM((2, 64, half), F32),
            pltpu.VMEM((STATION_COUNT, 2 * total_b), BF16),
            pltpu.VMEM((2, chips * half, 128), F32),
            pltpu.VMEM((2, 128, STATION_COUNT), BF16),
            pltpu.VMEM((2, 128, half), F32),
            pltpu.VMEM((2, 256, 2 * total_b), BF16),
            pltpu.VMEM((2, chips, size, 128), F32),
            pltpu.VMEM((2, peers, size, 128), F32),
            pltpu.VMEM((8, 128), F32),
            pltpu.VMEM((8, 128), F32),
            pltpu.VMEM((peers, 8, 128), F32),
            pltpu.VMEM((2 * nch - 1, 8, 128), F32),
            pltpu.VMEM((3, 2, 2, half, 128), F32),
            dma((5,)),
            dma((4,)),
            dma((4,)),
            dma((2, peers)),
            dma((2, peers)),
            dma((2, peers)),
            dma((2, peers)),
            dma((2, 5)),
            dma((3, 2, 2)),
            dma((peers,)),
            dma((peers,)),
            dma((2 * nch - 1,)),
            dma((2 * nch - 1,)),
        ],
        compiler_params=pltpu.CompilerParams(
            collective_id=0, has_side_effects=True, vmem_limit_bytes=48 * 1024 * 1024),
    )(visibilities, model, first_station[None], second_station[None], gain_offset)
    smoothed = jnp.transpose(smooth.reshape(4, 8, 8, half), (2, 1, 0, 3))
    count_vis = 8.0 * nb * lax.axis_size("bl") * 4 * nch
    misfit = chi[:ITERS, 0] / count_vis
    return (smoothed, misfit)


def solution(mesh):
    return jax.shard_map(
        on_device,
        mesh=mesh,
        in_specs=(
            P(None, "ch", "bl"),
            P(None, None, "ch", "bl"),
            P("bl"),
            P("bl"),
            P(None, None, "ch", "bl"),
        ),
        out_specs=(P(None, None, "ch", "bl"), P()),
        check_vma=False,
    )
```

```python
import functools

import jax
import jax.numpy as jnp
from jax import lax
from jax.experimental import pallas as pl
from jax.experimental.pallas import tpu as pltpu
from jax.sharding import PartitionSpec as P

STATION_COUNT = 512
ITERS = 3
SPAN = 4
REG = 1.0
KERNEL_VAR = 4.0
BLOCK = 256
F32 = jnp.float32
BF16 = jnp.bfloat16


def cmul(a, b):
    return (a[0] * b[0] - a[1] * b[1], a[0] * b[1] + a[1] * b[0])


def cadd(a, b):
    return (a[0] + b[0], a[1] + b[1])


def conj(a):
    return (a[0], -a[1])


def matmul22(a, b):
    return [
        cadd(cmul(a[0], b[0]), cmul(a[1], b[2])),
        cadd(cmul(a[0], b[1]), cmul(a[1], b[3])),
        cadd(cmul(a[2], b[0]), cmul(a[3], b[2])),
        cadd(cmul(a[2], b[1]), cmul(a[3], b[3])),
    ]


def herm(a):
    return [conj(a[0]), conj(a[2]), conj(a[1]), conj(a[3])]


def gram_parts(y):
    diag_one = y[0][0] ** 2 + y[0][1] ** 2 + y[1][0] ** 2 + y[1][1] ** 2
    diag_two = y[2][0] ** 2 + y[2][1] ** 2 + y[3][0] ** 2 + y[3][1] ** 2
    off = cadd(cmul(y[0], conj(y[2])), cmul(y[1], conj(y[3])))
    return [diag_one, diag_two, off[0], off[1]]


def flat(m):
    return [m[k][j] for k in range(4) for j in range(2)]


def pairs(parts):
    return [(parts[2 * k], parts[2 * k + 1]) for k in range(4)]


def nt_dot(a, b):
    return lax.dot_general(a, b, (((1,), (1,)), ((), ())), preferred_element_type=F32)


def plane(chips):
    ny = 1
    while ny * ny < chips:
        ny *= 2
    return (chips // ny, ny)


def far_first(chips):
    nx, ny = plane(chips)

    def hops(o):
        return min(o[0], nx - o[0]) + min(o[1], ny - o[1])

    others = [(i, j) for i in range(nx) for j in range(ny) if i + j > 0]
    return sorted(others, key=lambda o: -hops(o))


def kernel(
    chips,
    nch,
    vis_hbm,
    model_hbm,
    first_hbm,
    second_hbm,
    goff_hbm,
    out_ref,
    chi_ref,
    vis_in,
    model_in,
    first_in,
    second_in,
    goff_in,
    m_all,
    m_stage,
    v_all,
    v_stage,
    s_all,
    g_stage,
    onehot,
    gains,
    gains_hl,
    own_t,
    term,
    norm,
    recv,
    chi_acc,
    chi_plane,
    chi_xy,
    chi_z,
    fin,
    in_sem,
    ex_send,
    ex_recv,
    rs_send,
    rs_recv,
    ag_send,
    ag_recv,
    fin_send,
    fin_recv,
    xy_send,
    xy_recv,
    z_send,
    z_recv,
):
    nb = vis_in.shape[2]
    total_b = 2 * nb
    half = goff_in.shape[3]
    quarter = half // 2
    side = chips * half
    size = half + quarter
    nx, ny = plane(chips)
    offsets = far_first(chips)
    peers = len(offsets)
    me = lax.axis_index("bl")
    z = lax.axis_index("ch")
    chip = me // 2
    core = me % 2
    sib = chip * 2 + (1 - core)
    px = chip // ny
    py = chip % ny
    lanes = 128

    def there(bl, ch=None):
        return {"bl": bl, "ch": z if ch is None else ch}

    def peer(k):
        return ((px + offsets[k][0]) % nx) * ny + (py + offsets[k][1]) % ny

    def send(src, dst, ssem, rsem, where):
        return pltpu.make_async_remote_copy(
            src_ref=src, dst_ref=dst, send_sem=ssem, recv_sem=rsem,
            device_id=where, device_id_type=pl.DeviceIdType.MESH)

    def along_z(k):
        return there(chip * 2 + (core + k) % 2, (z + k // 2) % nch)

    z_order = sorted(range(1, 2 * nch), key=lambda k: -min(k // 2, nch - k // 2))

    barrier = pltpu.get_barrier_semaphore()
    for k in z_order:
        pl.semaphore_signal(barrier, inc=1, device_id=along_z(k),
                            device_id_type=pl.DeviceIdType.MESH)
    for k in range(peers):
        pl.semaphore_signal(barrier, inc=1, device_id=there(peer(k) * 2 + core),
                            device_id_type=pl.DeviceIdType.MESH)

    loads = [
        pltpu.make_async_copy(goff_hbm, goff_in, in_sem.at[0]),
        pltpu.make_async_copy(model_hbm, model_in, in_sem.at[1]),
        pltpu.make_async_copy(vis_hbm, vis_in, in_sem.at[2]),
        pltpu.make_async_copy(first_hbm, first_in, in_sem.at[3]),
        pltpu.make_async_copy(second_hbm, second_in, in_sem.at[4]),
    ]
    for load in loads:
        load.start()

    r = lax.broadcasted_iota(jnp.int32, (256, 256), 0)
    q = lax.broadcasted_iota(jnp.int32, (256, 256), 1)
    chan = 2 * ((core + r // 128) & 1) + (r // 64) % 2
    perm = jnp.where(q == (r % 8) * 32 + ((r // 8) % 8) * 4 + chan, 1.0, 0.0).astype(BF16)

    loads[0].wait()
    offs = goff_in[...].reshape(256, half)
    hi = offs.astype(BF16)
    rest = offs - hi.astype(F32)
    mid = rest.astype(BF16)
    low = (rest - mid.astype(F32)).astype(BF16)
    turned = [jnp.dot(perm, one, preferred_element_type=F32) for one in (hi, mid, low)]
    comp = (lax.broadcasted_iota(jnp.int32, (256, half), 0) // 8) % 8
    start = jnp.where((comp == 0) | (comp == 6), 1.0, 0.0) + ((turned[0] + turned[1]) + turned[2])
    here_rows = pl.ds(pl.multiple_of(core * 64, 64), 64)
    for c in range(2):
        own_t[c, here_rows, :] = start[c * 64:c * 64 + 64]
        g_stage[c] = start[128 + c * 64:192 + c * 64]

    loads[1].wait()
    permuted = jnp.dot(perm, model_in[...].reshape(256, nb), preferred_element_type=F32)
    m_all[:, :nb] = permuted[:128]
    m_stage[...] = permuted[128:]
    loads[2].wait()
    for c in range(2):
        for k in range(8):
            row = c * 8 + k
            v_all[row:row + 1, :nb] = vis_in[k, pl.ds(2 * core + c, 1), :]
            v_stage[row:row + 1, :] = vis_in[k, pl.ds(2 * (1 - core) + c, 1), :]
    loads[3].wait()
    loads[4].wait()

    def place(s):
        rem = s % (2 * half)
        return (rem // half) * side + (s // (2 * half)) * half + rem % half

    s_all[0, 0:1, :] = place(first_in[...])
    s_all[0, 1:2, :] = place(second_in[...])
    s_all[0, 2:8, :] = jnp.zeros((6, nb), jnp.int32)

    station = lax.broadcasted_iota(jnp.int32, (STATION_COUNT, BLOCK), 0)

    def hot(part):
        def body(i, carry):
            at = pl.multiple_of(i * BLOCK, BLOCK)
            for j in range(2):
                which = s_all[part, j:j + 1, pl.ds(at, BLOCK)]
                to = pl.multiple_of(j * total_b + part * nb + at, BLOCK)
                onehot[:, pl.ds(to, BLOCK)] = jnp.where(station == which, 1.0, 0.0).astype(BF16)
            return carry

        lax.fori_loop(0, nb // BLOCK, body, 0)

    chi_acc[...] = jnp.zeros_like(chi_acc)
    pl.semaphore_wait(barrier, 2 * nch - 1 + peers)

    swaps = [
        send(g_stage, own_t.at[:, here_rows, :], ex_send.at[0], ex_recv.at[0], there(sib)),
        send(s_all.at[0], s_all.at[1], ex_send.at[1], ex_recv.at[1], there(sib)),
        send(m_stage, m_all.at[:, pl.ds(nb, nb)], ex_send.at[2], ex_recv.at[2], there(sib)),
        send(v_stage, v_all.at[:, pl.ds(nb, nb)], ex_send.at[3], ex_recv.at[3], there(sib)),
    ]
    for swap in swaps:
        swap.start()
    chip_rows = pl.ds(pl.multiple_of(chip * half, half), half)

    def ag_copy(c, k):
        return send(gains.at[c, chip_rows, :], gains.at[c, chip_rows, :],
                    ag_send.at[c, k], ag_recv.at[c, k], there(peer(k) * 2 + core))

    swaps[0].wait_recv()
    for c in range(2):
        gains[c, chip_rows, :] = jnp.transpose(own_t[c])
        for k in range(peers):
            ag_copy(c, k).start()
    hot(0)
    swaps[1].wait_recv()
    hot(1)
    swaps[2].wait_recv()
    swaps[3].wait_recv()
    for swap in swaps:
        swap.wait_send()

    def store_pair(c, row, cols, one, two):
        both = jnp.concatenate([one, two], axis=0)
        hi = both.astype(BF16)
        term[c, row:row + 16, cols] = hi
        term[c, 128 + row:144 + row, cols] = (both - hi.astype(F32)).astype(BF16)

    def terms(c, step):
        both = gains_hl[c]
        chi = jnp.zeros((1, lanes), F32)
        for i in range(total_b // BLOCK):
            cols = pl.ds(i * BLOCK, BLOCK)
            cols_q = pl.ds(total_b + i * BLOCK, BLOCK)
            gp = jnp.dot(both, onehot[:, cols], preferred_element_type=F32)
            gp = gp[:64] + gp[64:]
            gq = jnp.dot(both, onehot[:, cols_q], preferred_element_type=F32)
            gq = gq[:64] + gq[64:]

            def part(x):
                return pairs([x[8 * k:8 * k + 8] for k in range(8)])

            jp = part(gp)
            jq = part(gq)
            mod = pairs([m_all[c * 64 + 8 * k:c * 64 + 8 * k + 8, cols] for k in range(8)])
            y_one = matmul22(mod, herm(jq))
            pred = flat(matmul22(jp, y_one))
            y_two = matmul22(herm(mod), herm(jp))
            resid = []
            for k in range(8):
                one = v_all[c * 8 + k:c * 8 + k + 1, cols] - jnp.sum(pred[k], axis=0, keepdims=True)
                for j in range(0, BLOCK, lanes):
                    chi = chi + one[:, j:j + lanes] * one[:, j:j + lanes]
                resid.append(one)
            resid = pairs(resid)
            a_one = flat(matmul22(resid, herm(y_one))) + gram_parts(y_one)
            a_two = flat(matmul22(herm(resid), herm(y_two))) + gram_parts(y_two)
            for k in range(0, 12, 2):
                store_pair(c, 8 * k, cols, a_one[k], a_one[k + 1])
                store_pair(c, 8 * k, cols_q, a_two[k], a_two[k + 1])
        chi_acc[pl.ds(step, 1), :] += chi

    lane_a = lax.broadcasted_iota(jnp.int32, (side, lanes), 1)
    lane_b = lax.broadcasted_iota(jnp.int32, (quarter, lanes), 1)

    def rs_copy(c, k):
        return send(norm.at[c, peer(k)], recv.at[c, k], rs_send.at[c, k], rs_recv.at[c, k],
                    there(peer(k) * 2 + core))

    def scatter(c):
        sums = nt_dot(onehot[...], term[c])
        sums = sums[:, :lanes] + sums[:, lanes:]
        lower = sums[:side]
        upper = pltpu.roll(sums[side:], 64, 1)
        packed = jnp.where(lane_a < 64, lower, upper)
        for j in range(chips):
            norm[c, j, :half, :] = packed[j * half:(j + 1) * half]
            mid_row = j * half + quarter
            end = (j + 1) * half
            low_one = lower[j * half:mid_row]
            low_two = pltpu.roll(lower[mid_row:end], 32, 1)
            up_one = upper[j * half:mid_row]
            up_two = pltpu.roll(upper[mid_row:end], 32, 1)
            norm[c, j, half:size, :] = jnp.where(
                lane_b < 64,
                jnp.where(lane_b < 32, up_one, up_two),
                jnp.where(lane_b < 96, low_one, low_two))
        for k in range(peers):
            rs_copy(c, k).start()

    def solve(c):
        total = norm[c, chip]
        for k in reversed(range(peers)):
            rs_copy(c, k).wait_recv()
            total = total + recv[c, k]
        r_t = jnp.transpose(total[:half])
        b_t = jnp.transpose(jnp.concatenate(
            [total[half:], pltpu.roll(total[half:], 96, 1)], axis=0))
        fresh_rows = []
        for h in range(2):
            old = [own_t[c, h * 64 + 8 * k:h * 64 + 8 * k + 8, :] for k in range(8)]
            amat = pairs([r_t[h * 64 + 8 * k:h * 64 + 8 * k + 8, :] - old[k] for k in range(8)])
            base = 64 * (1 - h)
            diag_one, diag_two, off_re, off_im = [
                b_t[base + 8 * k:base + 8 * k + 8, :] for k in range(4)]
            diag_one = diag_one + REG
            diag_two = diag_two + REG
            det = diag_one * diag_two - off_re * off_re - off_im * off_im
            scale = 0.5 / det
            d_one = diag_one * scale
            d_two = diag_two * scale
            o_re = off_re * scale
            o_im = off_im * scale
            for row in range(2):
                a0 = amat[2 * row]
                a1 = amat[2 * row + 1]
                n0 = cadd((a0[0] * d_two, a0[1] * d_two), cmul(a1, (-o_re, o_im)))
                n1 = cadd(cmul(a0, (-o_re, -o_im)), (a1[0] * d_one, a1[1] * d_one))
                k = 4 * row
                fresh_rows += [old[k] + n0[0], old[k + 1] + n0[1],
                               old[k + 2] + n1[0], old[k + 3] + n1[1]]
        fresh = jnp.concatenate(fresh_rows, axis=0)
        own_t[c] = fresh
        return jnp.transpose(fresh)

    def prepare(c):
        for k in reversed(range(peers)):
            ag_copy(c, k).wait_recv()
        turned = jnp.transpose(gains[c])
        turned = jnp.concatenate([turned[:64], turned[64:]], axis=1)
        hi = turned.astype(BF16)
        gains_hl[c, :64] = hi
        gains_hl[c, 64:] = (turned - hi.astype(F32)).astype(BF16)

    def after_scatter(c):
        for k in range(peers):
            ag_copy(c, k).wait_send()

    def after_solve(c):
        for k in range(peers):
            rs_copy(c, k).wait_send()

    def early(step, carry):
        for c in range(2):
            prepare(c)
            terms(c, step)
            scatter(c)
            after_scatter(c)
        for c in range(2):
            gains[c, chip_rows, :] = solve(c)
            for k in range(peers):
                ag_copy(c, k).start()
            after_solve(c)
        return carry

    lax.fori_loop(0, ITERS - 1, early, 0)

    def xy_copy(k):
        return send(chi_acc, chi_xy.at[k], xy_send.at[k], xy_recv.at[k],
                    there(peer(k) * 2 + core))

    def z_copy(k):
        return send(chi_plane, chi_z.at[k - 1], z_send.at[k - 1], z_recv.at[k - 1], along_z(k))

    def up(c, which):
        return send(fin.at[1, core, c], fin.at[0, core, c], fin_send.at[c, which],
                    fin_recv.at[0, core, c], there(chip * 2 + which, (z + 1) % nch))

    def down(c, which):
        return send(fin.at[1, core, c], fin.at[2, core, c], fin_send.at[c, 2 + which],
                    fin_recv.at[2, core, c], there(chip * 2 + which, (z + nch - 1) % nch))

    def across(c):
        return send(fin.at[1, core, c], fin.at[1, core, c], fin_send.at[c, 4],
                    fin_recv.at[1, core, c], there(sib))

    def halo(c):
        fin[1, core, c] = solve(c)

        @pl.when(z < nch - 1)
        def _():
            for which in range(2):
                up(c, which).start()

        @pl.when(z > 0)
        def _():
            for which in range(2):
                down(c, which).start()

        across(c).start()

    for c in range(2):
        prepare(c)
        terms(c, ITERS - 1)
        if c == 1:
            for k in range(peers):
                xy_copy(k).start()
        scatter(c)
        after_scatter(c)

    @pl.when(z == 0)
    def _():
        fin[0] = jnp.zeros(fin.shape[1:], F32)

    @pl.when(z == nch - 1)
    def _():
        fin[2] = jnp.zeros(fin.shape[1:], F32)

    shape = (12 * half, 4 * lanes)
    row = lax.broadcasted_iota(jnp.int32, shape, 0)
    col = lax.broadcasted_iota(jnp.int32, shape, 1)
    to = col // lanes
    shift = row // half - 4 - to

    def weigh(step):
        step = step.astype(F32)
        return jnp.exp(-(step * step) / (2.0 * KERNEL_VAR))

    line = lax.broadcasted_iota(jnp.int32, (1, 4 * lanes), 1) // lanes
    denom = jnp.zeros((1, 4 * lanes), F32)
    for s in range(-SPAN, SPAN + 1):
        at = z * 4 + line + s
        denom = denom + jnp.where((at >= 0) & (at < 4 * nch), weigh(jnp.full((1, 4 * lanes), s, jnp.int32)), 0.0)
    mixing = jnp.where(
        (row % half == col % lanes) & (shift >= -SPAN) & (shift <= SPAN), weigh(shift) / denom, 0.0)

    halo(0)
    chi = chi_acc[...]
    for k in reversed(range(peers)):
        xy_copy(k).wait_recv()
        chi = chi + chi_xy[k]
    chi_plane[...] = chi
    for k in z_order:
        z_copy(k).start()
    halo(1)
    for c in range(2):
        after_solve(c)

    def wait_fin(slot, source):
        for c in range(2):
            send(fin.at[slot, source, c], fin.at[slot, source, c], fin_send.at[c, 0],
                 fin_recv.at[slot, source, c], there(sib)).wait_recv()

    wait_fin(1, 1 - core)

    @pl.when(z > 0)
    def _():
        for source in range(2):
            wait_fin(0, source)

    @pl.when(z < nch - 1)
    def _():
        for source in range(2):
            wait_fin(2, source)

    slabs = jnp.transpose(fin[...].reshape(12 * half, lanes))
    slabs = jnp.where(core == 0, slabs[:64], slabs[64:])
    smooth = jnp.dot(slabs, mixing, precision=lax.Precision.HIGHEST, preferred_element_type=F32)
    for c in range(4):
        out_ref[c] = smooth[:, c * lanes:c * lanes + half]

    chi = chi_plane[...]
    for k in reversed(z_order):
        z_copy(k).wait_recv()
        chi = chi + chi_z[k - 1]
    chi_ref[...] = jnp.broadcast_to(jnp.sum(chi, axis=1, keepdims=True), (8, lanes))

    for k in range(peers):
        xy_copy(k).wait_send()
    for k in z_order:
        z_copy(k).wait_send()
    for c in range(2):
        across(c).wait_send()

    @pl.when(z < nch - 1)
    def _():
        for c in range(2):
            for which in range(2):
                up(c, which).wait_send()

    @pl.when(z > 0)
    def _():
        for c in range(2):
            for which in range(2):
                down(c, which).wait_send()


def on_device(visibilities, model, first_station, second_station, gain_offset):
    nb = visibilities.shape[2]
    half = gain_offset.shape[3]
    chips = lax.axis_size("bl") // 2
    nch = lax.axis_size("ch")
    size = half + half // 2
    total_b = 2 * nb
    peers = chips - 1
    vmem = pl.BlockSpec(memory_space=pltpu.VMEM)
    hbm = pl.BlockSpec(memory_space=pltpu.HBM)
    dma = pltpu.SemaphoreType.DMA
    smooth, chi = pl.pallas_call(
        functools.partial(kernel, chips, nch),
        out_shape=(
            jax.ShapeDtypeStruct((4, 64, half), F32),
            jax.ShapeDtypeStruct((8, 128), F32),
        ),
        in_specs=[hbm] * 5,
        out_specs=(vmem, vmem),
        scratch_shapes=[
            pltpu.VMEM(visibilities.shape, F32),
            pltpu.VMEM(model.shape, BF16),
            pltpu.VMEM((1, nb), jnp.int32),
            pltpu.VMEM((1, nb), jnp.int32),
            pltpu.VMEM(gain_offset.shape, F32),
            pltpu.VMEM((128, total_b), F32),
            pltpu.VMEM((128, nb), F32),
            pltpu.VMEM((16, total_b), F32),
            pltpu.VMEM((16, nb), F32),
            pltpu.VMEM((2, 8, nb), jnp.int32),
            pltpu.VMEM((2, 64, half), F32),
            pltpu.VMEM((STATION_COUNT, 2 * total_b), BF16),
            pltpu.VMEM((2, chips * half, 128), F32),
            pltpu.VMEM((2, 128, STATION_COUNT), BF16),
            pltpu.VMEM((2, 128, half), F32),
            pltpu.VMEM((2, 256, 2 * total_b), BF16),
            pltpu.VMEM((2, chips, size, 128), F32),
            pltpu.VMEM((2, peers, size, 128), F32),
            pltpu.VMEM((8, 128), F32),
            pltpu.VMEM((8, 128), F32),
            pltpu.VMEM((peers, 8, 128), F32),
            pltpu.VMEM((2 * nch - 1, 8, 128), F32),
            pltpu.VMEM((3, 2, 2, half, 128), F32),
            dma((5,)),
            dma((4,)),
            dma((4,)),
            dma((2, peers)),
            dma((2, peers)),
            dma((2, peers)),
            dma((2, peers)),
            dma((2, 5)),
            dma((3, 2, 2)),
            dma((peers,)),
            dma((peers,)),
            dma((2 * nch - 1,)),
            dma((2 * nch - 1,)),
        ],
        compiler_params=pltpu.CompilerParams(
            collective_id=0, has_side_effects=True, vmem_limit_bytes=48 * 1024 * 1024),
    )(*[pltpu.with_memory_space_constraint(x, pltpu.HBM) for x in (visibilities, model, first_station[None], second_station[None], gain_offset)])
    smoothed = jnp.transpose(smooth.reshape(4, 8, 8, half), (2, 1, 0, 3))
    count_vis = 8.0 * nb * lax.axis_size("bl") * 4 * nch
    misfit = chi[:ITERS, 0] / count_vis
    return (smoothed, misfit)


def solution(mesh):
    return jax.shard_map(
        on_device,
        mesh=mesh,
        in_specs=(
            P(None, "ch", "bl"),
            P(None, None, "ch", "bl"),
            P("bl"),
            P("bl"),
            P(None, None, "ch", "bl"),
        ),
        out_specs=(P(None, None, "ch", "bl"), P()),
        check_vma=False,
    )
```

```python
import functools

import jax
import jax.numpy as jnp
from jax import lax
from jax.experimental import pallas as pl
from jax.experimental.pallas import tpu as pltpu
from jax.sharding import PartitionSpec as P

STATION_COUNT = 512
ITERS = 3
SPAN = 4
REG = 1.0
KERNEL_VAR = 4.0
BLOCK = 256
HELD = 3
F32 = jnp.float32
BF16 = jnp.bfloat16


def cmul(a, b):
    return (a[0] * b[0] - a[1] * b[1], a[0] * b[1] + a[1] * b[0])


def cadd(a, b):
    return (a[0] + b[0], a[1] + b[1])


def conj(a):
    return (a[0], -a[1])


def matmul22(a, b):
    return [
        cadd(cmul(a[0], b[0]), cmul(a[1], b[2])),
        cadd(cmul(a[0], b[1]), cmul(a[1], b[3])),
        cadd(cmul(a[2], b[0]), cmul(a[3], b[2])),
        cadd(cmul(a[2], b[1]), cmul(a[3], b[3])),
    ]


def herm(a):
    return [conj(a[0]), conj(a[2]), conj(a[1]), conj(a[3])]


def gram_parts(y):
    diag_one = y[0][0] ** 2 + y[0][1] ** 2 + y[1][0] ** 2 + y[1][1] ** 2
    diag_two = y[2][0] ** 2 + y[2][1] ** 2 + y[3][0] ** 2 + y[3][1] ** 2
    off = cadd(cmul(y[0], conj(y[2])), cmul(y[1], conj(y[3])))
    return [diag_one, diag_two, off[0], off[1]]


def flat(m):
    return [m[k][j] for k in range(4) for j in range(2)]


def pairs(parts):
    return [(parts[2 * k], parts[2 * k + 1]) for k in range(4)]


def nt_dot(a, b):
    return lax.dot_general(a, b, (((1,), (1,)), ((), ())), preferred_element_type=F32)


def plane(chips):
    ny = 1
    while ny * ny < chips:
        ny *= 2
    return (chips // ny, ny)


def far_first(chips):
    nx, ny = plane(chips)

    def hops(o):
        return min(o[0], nx - o[0]) + min(o[1], ny - o[1])

    others = [(i, j) for i in range(nx) for j in range(ny) if i + j > 0]
    return sorted(others, key=lambda o: -hops(o))


def kernel(
    chips,
    nch,
    vis_hbm,
    model_hbm,
    first_hbm,
    second_hbm,
    goff_hbm,
    out_ref,
    chi_ref,
    vis_in,
    model_in,
    first_in,
    second_in,
    goff_in,
    m_all,
    m_stage,
    v_all,
    v_stage,
    s_all,
    g_stage,
    onehot,
    gains,
    gains_hl,
    own_t,
    term,
    norm,
    recv,
    chi_acc,
    chi_plane,
    chi_xy,
    chi_z,
    fin,
    in_sem,
    ex_send,
    ex_recv,
    rs_send,
    rs_recv,
    ag_send,
    ag_recv,
    fin_send,
    fin_recv,
    xy_send,
    xy_recv,
    z_send,
    z_recv,
):
    nb = vis_in.shape[2]
    total_b = 2 * nb
    half = goff_in.shape[3]
    quarter = half // 2
    side = chips * half
    size = half + quarter
    nx, ny = plane(chips)
    offsets = far_first(chips)
    peers = len(offsets)
    me = lax.axis_index("bl")
    z = lax.axis_index("ch")
    chip = me // 2
    core = me % 2
    sib = chip * 2 + (1 - core)
    px = chip // ny
    py = chip % ny
    lanes = 128

    def there(bl, ch=None):
        return {"bl": bl, "ch": z if ch is None else ch}

    def peer(k):
        return ((px + offsets[k][0]) % nx) * ny + (py + offsets[k][1]) % ny

    def send(src, dst, ssem, rsem, where):
        return pltpu.make_async_remote_copy(
            src_ref=src, dst_ref=dst, send_sem=ssem, recv_sem=rsem,
            device_id=where, device_id_type=pl.DeviceIdType.MESH)

    def along_z(k):
        return there(chip * 2 + (core + k) % 2, (z + k // 2) % nch)

    z_order = sorted(range(1, 2 * nch), key=lambda k: -min(k // 2, nch - k // 2))

    barrier = pltpu.get_barrier_semaphore()
    for k in z_order:
        pl.semaphore_signal(barrier, inc=1, device_id=along_z(k),
                            device_id_type=pl.DeviceIdType.MESH)
    for k in range(peers):
        pl.semaphore_signal(barrier, inc=1, device_id=there(peer(k) * 2 + core),
                            device_id_type=pl.DeviceIdType.MESH)

    loads = [
        pltpu.make_async_copy(goff_hbm, goff_in, in_sem.at[0]),
        pltpu.make_async_copy(model_hbm, model_in, in_sem.at[1]),
        pltpu.make_async_copy(vis_hbm, vis_in, in_sem.at[2]),
        pltpu.make_async_copy(first_hbm, first_in, in_sem.at[3]),
        pltpu.make_async_copy(second_hbm, second_in, in_sem.at[4]),
    ]
    for load in loads:
        load.start()

    def mine(c, work):
        if c == 0:
            work()
        else:
            pl.when(core == 1)(work)

    r = lax.broadcasted_iota(jnp.int32, (256, 256), 0)
    q = lax.broadcasted_iota(jnp.int32, (256, 256), 1)
    chan = (r // 64 + core) % 4
    perm = jnp.where(q == (r % 8) * 32 + ((r // 8) % 8) * 4 + chan, 1.0, 0.0).astype(BF16)

    loads[0].wait()
    offs = goff_in[...].reshape(256, half)
    hi = offs.astype(BF16)
    rest = offs - hi.astype(F32)
    mid = rest.astype(BF16)
    low = (rest - mid.astype(F32)).astype(BF16)
    turned = [jnp.dot(perm, one, preferred_element_type=F32) for one in (hi, mid, low)]
    comp = (lax.broadcasted_iota(jnp.int32, (256, half), 0) // 8) % 8
    start = jnp.where((comp == 0) | (comp == 6), 1.0, 0.0) + ((turned[0] + turned[1]) + turned[2])
    here_rows = pl.ds(pl.multiple_of(core * 64, 64), 64)
    for c in range(HELD):
        own_t[c, here_rows, :] = start[c * 64:c * 64 + 64]

    @pl.when(core == 0)
    def _():
        for c in range(HELD):
            g_stage[c] = start[(c + 1) * 64:(c + 2) * 64]

    @pl.when(core == 1)
    def _():
        g_stage[0] = start[192:]

    loads[1].wait()
    permuted = jnp.dot(perm, model_in[...].reshape(256, nb), preferred_element_type=F32)
    m_all[:, :nb] = permuted[:192]

    @pl.when(core == 0)
    def _():
        m_stage[...] = permuted[64:]

    @pl.when(core == 1)
    def _():
        m_stage[:64] = permuted[192:]

    loads[2].wait()
    for c in range(HELD):
        for k in range(8):
            row = c * 8 + k
            v_all[row:row + 1, :nb] = vis_in[k, pl.ds(core + c, 1), :]
            v_stage[row:row + 1, :] = vis_in[k, pl.ds(1 - core + c, 1), :]
    loads[3].wait()
    loads[4].wait()

    def place(s):
        rem = s % (2 * half)
        return (rem // half) * side + (s // (2 * half)) * half + rem % half

    s_all[0, 0:1, :] = place(first_in[...])
    s_all[0, 1:2, :] = place(second_in[...])
    s_all[0, 2:8, :] = jnp.zeros((6, nb), jnp.int32)

    def hot(part):
        for i in range(nb // BLOCK):
            for j in range(2):
                which = s_all[part, j:j + 1, i * BLOCK:(i + 1) * BLOCK]
                to = j * total_b + part * nb + i * BLOCK
                station = lax.broadcasted_iota(jnp.int32, (STATION_COUNT, BLOCK), 0)
                onehot[:, to:to + BLOCK] = jnp.where(station == which, 1.0, 0.0).astype(BF16)

    chi_acc[...] = jnp.zeros_like(chi_acc)
    pl.semaphore_wait(barrier, 2 * nch - 1 + peers)

    def swap_pair(count):
        return [
            send(g_stage.at[pl.ds(0, count)], own_t.at[pl.ds(0, count), here_rows, :],
                 ex_send.at[0], ex_recv.at[0], there(sib)),
            send(m_stage.at[pl.ds(0, count * 64)], m_all.at[pl.ds(0, count * 64), pl.ds(nb, nb)],
                 ex_send.at[2], ex_recv.at[2], there(sib)),
        ]

    give = {0: swap_pair(HELD), 1: swap_pair(1)}
    swaps = [
        send(s_all.at[0], s_all.at[1], ex_send.at[1], ex_recv.at[1], there(sib)),
        send(v_stage, v_all.at[:, pl.ds(nb, nb)], ex_send.at[3], ex_recv.at[3], there(sib)),
    ]

    def per_core(what):
        for which in range(2):
            @pl.when(core == which)
            def _():
                what(which)

    per_core(lambda which: [one.start() for one in give[which]] and None)
    for swap in swaps:
        swap.start()
    chip_rows = pl.ds(pl.multiple_of(chip * half, half), half)

    def ag_copy(c, k):
        return send(gains.at[c, chip_rows, :], gains.at[c, chip_rows, :],
                    ag_send.at[c], ag_recv.at[c], there(peer(k) * 2 + core))

    per_core(lambda which: give[1 - which][0].wait_recv())
    for c in range(HELD):
        def gather_start():
            gains[c, chip_rows, :] = jnp.transpose(own_t[c])
            for k in range(peers):
                ag_copy(c, k).start()

        mine(c, gather_start)
    hot(0)
    swaps[0].wait_recv()
    hot(1)
    per_core(lambda which: give[1 - which][1].wait_recv())
    swaps[1].wait_recv()
    per_core(lambda which: [one.wait_send() for one in give[which]] and None)
    for swap in swaps:
        swap.wait_send()

    def store_pair(c, row, cols, one, two):
        both = jnp.concatenate([one, two], axis=0)
        hi = both.astype(BF16)
        term[c, row:row + 16, cols] = hi
        term[c, 128 + row:144 + row, cols] = (both - hi.astype(F32)).astype(BF16)

    def terms(c, step):
        both = gains_hl[c]
        chi = jnp.zeros((1, lanes), F32)
        for i in range(total_b // BLOCK):
            cols = pl.ds(i * BLOCK, BLOCK)
            cols_q = pl.ds(total_b + i * BLOCK, BLOCK)
            gp = jnp.dot(both, onehot[:, cols], preferred_element_type=F32)
            gp = gp[:64] + gp[64:]
            gq = jnp.dot(both, onehot[:, cols_q], preferred_element_type=F32)
            gq = gq[:64] + gq[64:]

            def part(x):
                return pairs([x[8 * k:8 * k + 8] for k in range(8)])

            jp = part(gp)
            jq = part(gq)
            mod = pairs([m_all[c * 64 + 8 * k:c * 64 + 8 * k + 8, cols] for k in range(8)])
            y_one = matmul22(mod, herm(jq))
            pred = flat(matmul22(jp, y_one))
            y_two = matmul22(herm(mod), herm(jp))
            resid = []
            for k in range(8):
                one = v_all[c * 8 + k:c * 8 + k + 1, cols] - jnp.sum(pred[k], axis=0, keepdims=True)
                for j in range(0, BLOCK, lanes):
                    chi = chi + one[:, j:j + lanes] * one[:, j:j + lanes]
                resid.append(one)
            resid = pairs(resid)
            a_one = flat(matmul22(resid, herm(y_one))) + gram_parts(y_one)
            a_two = flat(matmul22(herm(resid), herm(y_two))) + gram_parts(y_two)
            for k in range(0, 12, 2):
                store_pair(c, 8 * k, cols, a_one[k], a_one[k + 1])
                store_pair(c, 8 * k, cols_q, a_two[k], a_two[k + 1])
        chi_acc[pl.ds(step, 1), :] += chi

    lane_a = lax.broadcasted_iota(jnp.int32, (side, lanes), 1)
    lane_b = lax.broadcasted_iota(jnp.int32, (quarter, lanes), 1)

    def rs_copy(c, k):
        return send(norm.at[c, peer(k)], recv.at[c, k], rs_send.at[c], rs_recv.at[c],
                    there(peer(k) * 2 + core))

    def scatter(c):
        sums = nt_dot(onehot[...], term[c])
        sums = sums[:, :lanes] + sums[:, lanes:]
        lower = sums[:side]
        upper = pltpu.roll(sums[side:], 64, 1)
        packed = jnp.where(lane_a < 64, lower, upper)
        for j in range(chips):
            norm[c, j, :half, :] = packed[j * half:(j + 1) * half]
            mid_row = j * half + quarter
            end = (j + 1) * half
            low_one = lower[j * half:mid_row]
            low_two = pltpu.roll(lower[mid_row:end], 32, 1)
            up_one = upper[j * half:mid_row]
            up_two = pltpu.roll(upper[mid_row:end], 32, 1)
            norm[c, j, half:size, :] = jnp.where(
                lane_b < 64,
                jnp.where(lane_b < 32, up_one, up_two),
                jnp.where(lane_b < 96, low_one, low_two))
        for k in range(peers):
            rs_copy(c, k).start()

    def rs_whole(c):
        return send(norm.at[c, pl.ds(0, peers)], recv.at[c], rs_send.at[c], rs_recv.at[c], there(sib))

    def ag_whole(c):
        part = gains.at[c, pl.ds(0, peers * half), :]
        return send(part, part, ag_send.at[c], ag_recv.at[c], there(sib))

    def solve(c):
        total = norm[c, chip]
        rs_whole(c).wait_recv()
        for k in range(peers):
            total = total + recv[c, k]
        r_t = jnp.transpose(total[:half])
        b_t = jnp.transpose(jnp.concatenate(
            [total[half:], pltpu.roll(total[half:], 96, 1)], axis=0))
        fresh_rows = []
        for h in range(2):
            old = [own_t[c, h * 64 + 8 * k:h * 64 + 8 * k + 8, :] for k in range(8)]
            amat = pairs([r_t[h * 64 + 8 * k:h * 64 + 8 * k + 8, :] - old[k] for k in range(8)])
            base = 64 * (1 - h)
            diag_one, diag_two, off_re, off_im = [
                b_t[base + 8 * k:base + 8 * k + 8, :] for k in range(4)]
            diag_one = diag_one + REG
            diag_two = diag_two + REG
            det = diag_one * diag_two - off_re * off_re - off_im * off_im
            scale = 0.5 / det
            d_one = diag_one * scale
            d_two = diag_two * scale
            o_re = off_re * scale
            o_im = off_im * scale
            for row in range(2):
                a0 = amat[2 * row]
                a1 = amat[2 * row + 1]
                n0 = cadd((a0[0] * d_two, a0[1] * d_two), cmul(a1, (-o_re, o_im)))
                n1 = cadd(cmul(a0, (-o_re, -o_im)), (a1[0] * d_one, a1[1] * d_one))
                k = 4 * row
                fresh_rows += [old[k] + n0[0], old[k + 1] + n0[1],
                               old[k + 2] + n1[0], old[k + 3] + n1[1]]
        fresh = jnp.concatenate(fresh_rows, axis=0)
        own_t[c] = fresh
        return jnp.transpose(fresh)

    def prepare(c):
        ag_whole(c).wait_recv()
        turned = jnp.transpose(gains[c])
        turned = jnp.concatenate([turned[:64], turned[64:]], axis=1)
        hi = turned.astype(BF16)
        gains_hl[c, :64] = hi
        gains_hl[c, 64:] = (turned - hi.astype(F32)).astype(BF16)

    def after_scatter(c):
        ag_whole(c).wait_send()

    def after_solve(c):
        rs_whole(c).wait_send()

    def early(step, carry):
        for c in range(HELD):
            def forth():
                prepare(c)
                terms(c, step)
                scatter(c)
                after_scatter(c)

            mine(c, forth)
        for c in range(HELD):
            def back():
                gains[c, chip_rows, :] = solve(c)
                for k in range(peers):
                    ag_copy(c, k).start()
                after_solve(c)

            mine(c, back)
        return carry

    lax.fori_loop(0, ITERS - 1, early, 0)

    def xy_copy(k):
        return send(chi_acc, chi_xy.at[k], xy_send.at[0], xy_recv.at[0],
                    there(peer(k) * 2 + core))

    def z_copy(k):
        return send(chi_plane, chi_z.at[k - 1], z_send.at[0], z_recv.at[0], along_z(k))

    def up(c, which):
        g = core + c
        return send(fin.at[1, g], fin.at[0, g], fin_send.at[c, which],
                    fin_recv.at[0, g], there(chip * 2 + which, (z + 1) % nch))

    def down(c, which):
        g = core + c
        return send(fin.at[1, g], fin.at[2, g], fin_send.at[c, 2 + which],
                    fin_recv.at[2, g], there(chip * 2 + which, (z + nch - 1) % nch))

    def across(c):
        g = core + c
        return send(fin.at[1, g], fin.at[1, g], fin_send.at[c, 4],
                    fin_recv.at[1, g], there(sib))

    def halo(c):
        fin[1, core + c] = solve(c)

        @pl.when(z < nch - 1)
        def _():
            for which in range(2):
                up(c, which).start()

        @pl.when(z > 0)
        def _():
            for which in range(2):
                down(c, which).start()

        across(c).start()

    def xy_start():
        for k in range(peers):
            xy_copy(k).start()

    for c in range(HELD):
        def forth():
            prepare(c)
            terms(c, ITERS - 1)
            if c == 0:
                pl.when(core == 0)(xy_start)
            if c == HELD - 1:
                xy_start()
            scatter(c)
            after_scatter(c)

        mine(c, forth)

    @pl.when(z == 0)
    def _():
        fin[0] = jnp.zeros(fin.shape[1:], F32)

    @pl.when(z == nch - 1)
    def _():
        fin[2] = jnp.zeros(fin.shape[1:], F32)

    shape = (12 * half, 4 * lanes)
    row = lax.broadcasted_iota(jnp.int32, shape, 0)
    col = lax.broadcasted_iota(jnp.int32, shape, 1)
    to = col // lanes
    shift = row // half - 4 - to

    def weigh(step):
        step = step.astype(F32)
        return jnp.exp(-(step * step) / (2.0 * KERNEL_VAR))

    line = lax.broadcasted_iota(jnp.int32, (1, 4 * lanes), 1) // lanes
    denom = jnp.zeros((1, 4 * lanes), F32)
    for s in range(-SPAN, SPAN + 1):
        at = z * 4 + line + s
        denom = denom + jnp.where((at >= 0) & (at < 4 * nch), weigh(jnp.full((1, 4 * lanes), s, jnp.int32)), 0.0)
    mixing = jnp.where(
        (row % half == col % lanes) & (shift >= -SPAN) & (shift <= SPAN), weigh(shift) / denom, 0.0)

    def plane_chi():
        chi = chi_acc[...]
        send(chi_xy, chi_xy, xy_send.at[0], xy_recv.at[0], there(sib)).wait_recv()
        for k in range(peers):
            chi = chi + chi_xy[k]
        chi_plane[...] = chi
        for k in z_order:
            z_copy(k).start()

    halo(0)

    @pl.when(core == 1)
    def _():
        halo(1)

    plane_chi()

    @pl.when(core == 1)
    def _():
        halo(2)

    for c in range(HELD):
        mine(c, lambda: after_solve(c))

    def wait_fin(slot, which):
        for g in which:
            send(fin.at[slot, g], fin.at[slot, g], fin_send.at[0, 0],
                 fin_recv.at[slot, g], there(sib)).wait_recv()

    per_core(lambda which: wait_fin(1, range(1, 4) if which == 0 else range(1)))

    @pl.when(z > 0)
    def _():
        wait_fin(0, range(4))

    @pl.when(z < nch - 1)
    def _():
        wait_fin(2, range(4))

    slabs = jnp.transpose(fin[...].reshape(12 * half, lanes))
    slabs = jnp.where(core == 0, slabs[:64], slabs[64:])
    smooth = jnp.dot(slabs, mixing, precision=lax.Precision.HIGHEST, preferred_element_type=F32)
    for c in range(4):
        out_ref[c] = smooth[:, c * lanes:c * lanes + half]

    chi = chi_plane[...]
    send(chi_z, chi_z, z_send.at[0], z_recv.at[0], there(sib)).wait_recv()
    for k in z_order:
        chi = chi + chi_z[k - 1]
    chi_ref[...] = jnp.broadcast_to(jnp.sum(chi, axis=1, keepdims=True), (8, lanes))

    send(chi_xy, chi_xy, xy_send.at[0], xy_recv.at[0], there(sib)).wait_send()
    send(chi_z, chi_z, z_send.at[0], z_recv.at[0], there(sib)).wait_send()
    for c in range(HELD):
        def finish():
            across(c).wait_send()

            @pl.when(z < nch - 1)
            def _():
                for which in range(2):
                    up(c, which).wait_send()

            @pl.when(z > 0)
            def _():
                for which in range(2):
                    down(c, which).wait_send()

        mine(c, finish)


def on_device(visibilities, model, first_station, second_station, gain_offset):
    nb = visibilities.shape[2]
    half = gain_offset.shape[3]
    chips = lax.axis_size("bl") // 2
    nch = lax.axis_size("ch")
    size = half + half // 2
    total_b = 2 * nb
    peers = chips - 1
    vmem = pl.BlockSpec(memory_space=pltpu.VMEM)
    hbm = pl.BlockSpec(memory_space=pltpu.HBM)
    dma = pltpu.SemaphoreType.DMA
    smooth, chi = pl.pallas_call(
        functools.partial(kernel, chips, nch),
        out_shape=(
            jax.ShapeDtypeStruct((4, 64, half), F32),
            jax.ShapeDtypeStruct((8, 128), F32),
        ),
        in_specs=[hbm] * 5,
        out_specs=(vmem, vmem),
        scratch_shapes=[
            pltpu.VMEM(visibilities.shape, F32),
            pltpu.VMEM(model.shape, BF16),
            pltpu.VMEM((1, nb), jnp.int32),
            pltpu.VMEM((1, nb), jnp.int32),
            pltpu.VMEM(gain_offset.shape, F32),
            pltpu.VMEM((64 * HELD, total_b), F32),
            pltpu.VMEM((64 * HELD, nb), F32),
            pltpu.VMEM((8 * HELD, total_b), F32),
            pltpu.VMEM((8 * HELD, nb), F32),
            pltpu.VMEM((2, 8, nb), jnp.int32),
            pltpu.VMEM((HELD, 64, half), F32),
            pltpu.VMEM((STATION_COUNT, 2 * total_b), BF16),
            pltpu.VMEM((HELD, chips * half, 128), F32),
            pltpu.VMEM((HELD, 128, STATION_COUNT), BF16),
            pltpu.VMEM((HELD, 128, half), F32),
            pltpu.VMEM((HELD, 256, 2 * total_b), BF16),
            pltpu.VMEM((HELD, chips, size, 128), F32),
            pltpu.VMEM((HELD, peers, size, 128), F32),
            pltpu.VMEM((8, 128), F32),
            pltpu.VMEM((8, 128), F32),
            pltpu.VMEM((peers, 8, 128), F32),
            pltpu.VMEM((2 * nch - 1, 8, 128), F32),
            pltpu.VMEM((3, 4, half, 128), F32),
            dma((5,)),
            dma((4,)),
            dma((4,)),
            dma((HELD,)),
            dma((HELD,)),
            dma((HELD,)),
            dma((HELD,)),
            dma((HELD, 5)),
            dma((3, 4)),
            dma((1,)),
            dma((1,)),
            dma((1,)),
            dma((1,)),
        ],
        compiler_params=pltpu.CompilerParams(
            collective_id=0, has_side_effects=True, vmem_limit_bytes=48 * 1024 * 1024),
    )(*[pltpu.with_memory_space_constraint(x, pltpu.HBM) for x in (visibilities, model, first_station[None], second_station[None], gain_offset)])
    smoothed = jnp.transpose(smooth.reshape(4, 8, 8, half), (2, 1, 0, 3))
    count_vis = 8.0 * nb * lax.axis_size("bl") * 4 * nch
    misfit = chi[:ITERS, 0] / count_vis
    return (smoothed, misfit)


def solution(mesh):
    return jax.shard_map(
        on_device,
        mesh=mesh,
        in_specs=(
            P(None, "ch", "bl"),
            P(None, None, "ch", "bl"),
            P("bl"),
            P("bl"),
            P(None, None, "ch", "bl"),
        ),
        out_specs=(P(None, None, "ch", "bl"), P()),
        check_vma=False,
    )
```

```python
import functools

import jax
import jax.numpy as jnp
from jax import lax
from jax.experimental import pallas as pl
from jax.experimental.pallas import tpu as pltpu
from jax.sharding import PartitionSpec as P

STATION_COUNT = 512
ITERS = 3
SPAN = 4
REG = 1.0
KERNEL_VAR = 4.0
BLOCK = 256
HELD = 3
F32 = jnp.float32
BF16 = jnp.bfloat16


def cmul(a, b):
    return (a[0] * b[0] - a[1] * b[1], a[0] * b[1] + a[1] * b[0])


def cadd(a, b):
    return (a[0] + b[0], a[1] + b[1])


def conj(a):
    return (a[0], -a[1])


def matmul22(a, b):
    return [
        cadd(cmul(a[0], b[0]), cmul(a[1], b[2])),
        cadd(cmul(a[0], b[1]), cmul(a[1], b[3])),
        cadd(cmul(a[2], b[0]), cmul(a[3], b[2])),
        cadd(cmul(a[2], b[1]), cmul(a[3], b[3])),
    ]


def herm(a):
    return [conj(a[0]), conj(a[2]), conj(a[1]), conj(a[3])]


def gram_parts(y):
    diag_one = y[0][0] ** 2 + y[0][1] ** 2 + y[1][0] ** 2 + y[1][1] ** 2
    diag_two = y[2][0] ** 2 + y[2][1] ** 2 + y[3][0] ** 2 + y[3][1] ** 2
    off = cadd(cmul(y[0], conj(y[2])), cmul(y[1], conj(y[3])))
    return [diag_one, diag_two, off[0], off[1]]


def flat(m):
    return [m[k][j] for k in range(4) for j in range(2)]


def pairs(parts):
    return [(parts[2 * k], parts[2 * k + 1]) for k in range(4)]


def nt_dot(a, b):
    return lax.dot_general(a, b, (((1,), (1,)), ((), ())), preferred_element_type=F32)


def plane(chips):
    ny = 1
    while ny * ny < chips:
        ny *= 2
    return (chips // ny, ny)


def far_first(chips):
    nx, ny = plane(chips)

    def hops(o):
        return min(o[0], nx - o[0]) + min(o[1], ny - o[1])

    others = [(i, j) for i in range(nx) for j in range(ny) if i + j > 0]
    return sorted(others, key=lambda o: -hops(o))


def kernel(
    chips,
    nch,
    vis_hbm,
    model_hbm,
    first_hbm,
    second_hbm,
    goff_hbm,
    out_ref,
    chi_ref,
    vis_in,
    model_in,
    first_in,
    second_in,
    goff_in,
    m_all,
    m_stage,
    v_all,
    v_stage,
    s_all,
    g_stage,
    onehot,
    gains,
    gains_hl,
    own_t,
    term,
    norm,
    recv,
    chi_acc,
    chi_plane,
    chi_xy,
    chi_z,
    fin,
    in_sem,
    ex_send,
    ex_recv,
    rs_send,
    rs_recv,
    ag_send,
    ag_recv,
    fin_send,
    fin_recv,
    xy_send,
    xy_recv,
    z_send,
    z_recv,
):
    nb = vis_in.shape[2]
    total_b = 2 * nb
    half = goff_in.shape[3]
    quarter = half // 2
    side = chips * half
    size = half + quarter
    nx, ny = plane(chips)
    offsets = far_first(chips)
    peers = len(offsets)
    me = lax.axis_index("bl")
    z = lax.axis_index("ch")
    chip = me // 2
    core = me % 2
    sib = chip * 2 + (1 - core)
    px = chip // ny
    py = chip % ny
    lanes = 128

    def there(bl, ch=None):
        return {"bl": bl, "ch": z if ch is None else ch}

    def peer(k):
        return ((px + offsets[k][0]) % nx) * ny + (py + offsets[k][1]) % ny

    def send(src, dst, ssem, rsem, where):
        return pltpu.make_async_remote_copy(
            src_ref=src, dst_ref=dst, send_sem=ssem, recv_sem=rsem,
            device_id=where, device_id_type=pl.DeviceIdType.MESH)

    def along_z(k):
        return there(chip * 2 + (core + k) % 2, (z + k // 2) % nch)

    z_order = sorted(range(1, 2 * nch), key=lambda k: -min(k // 2, nch - k // 2))

    barrier = pltpu.get_barrier_semaphore()
    for k in range(peers):
        pl.semaphore_signal(barrier, inc=1, device_id=there(peer(k) * 2 + core),
                            device_id_type=pl.DeviceIdType.MESH)
    for k in z_order:
        pl.semaphore_signal(barrier, inc=1, device_id=along_z(k),
                            device_id_type=pl.DeviceIdType.MESH)

    loads = [
        pltpu.make_async_copy(goff_hbm, goff_in, in_sem.at[0]),
        pltpu.make_async_copy(model_hbm, model_in, in_sem.at[1]),
        pltpu.make_async_copy(vis_hbm, vis_in, in_sem.at[2]),
        pltpu.make_async_copy(first_hbm, first_in, in_sem.at[3]),
        pltpu.make_async_copy(second_hbm, second_in, in_sem.at[4]),
    ]
    for load in loads:
        load.start()

    def mine(c, work):
        if c == 0:
            work()
        else:
            pl.when(core == 1)(work)

    r = lax.broadcasted_iota(jnp.int32, (256, 256), 0)
    q = lax.broadcasted_iota(jnp.int32, (256, 256), 1)
    chan = (r // 64 + core) % 4
    perm = jnp.where(q == (r % 8) * 32 + ((r // 8) % 8) * 4 + chan, 1.0, 0.0).astype(BF16)

    loads[0].wait()
    offs = goff_in[...].reshape(256, half)
    hi = offs.astype(BF16)
    rest = offs - hi.astype(F32)
    mid = rest.astype(BF16)
    low = (rest - mid.astype(F32)).astype(BF16)
    turned = [jnp.dot(perm, one, preferred_element_type=F32) for one in (hi, mid, low)]
    comp = (lax.broadcasted_iota(jnp.int32, (256, half), 0) // 8) % 8
    start = jnp.where((comp == 0) | (comp == 6), 1.0, 0.0) + ((turned[0] + turned[1]) + turned[2])
    here_rows = pl.ds(pl.multiple_of(core * 64, 64), 64)
    for c in range(HELD):
        own_t[c, here_rows, :] = start[c * 64:c * 64 + 64]

    @pl.when(core == 0)
    def _():
        for c in range(HELD):
            g_stage[c] = start[(c + 1) * 64:(c + 2) * 64]

    @pl.when(core == 1)
    def _():
        g_stage[0] = start[192:]

    loads[1].wait()
    permuted = jnp.dot(perm, model_in[...].reshape(256, nb), preferred_element_type=F32)
    m_all[:, :nb] = permuted[:192]

    @pl.when(core == 0)
    def _():
        m_stage[...] = permuted[64:]

    @pl.when(core == 1)
    def _():
        m_stage[:64] = permuted[192:]

    loads[2].wait()
    for c in range(HELD):
        for k in range(8):
            row = c * 8 + k
            v_all[row:row + 1, :nb] = vis_in[k, pl.ds(core + c, 1), :]
            v_stage[row:row + 1, :] = vis_in[k, pl.ds(1 - core + c, 1), :]
    loads[3].wait()
    loads[4].wait()

    def place(s):
        rem = s % (2 * half)
        return (rem // half) * side + (s // (2 * half)) * half + rem % half

    s_all[0, 0:1, :] = place(first_in[...])
    s_all[0, 1:2, :] = place(second_in[...])
    s_all[0, 2:8, :] = jnp.zeros((6, nb), jnp.int32)

    def hot(part):
        for i in range(nb // BLOCK):
            for j in range(2):
                which = s_all[part, j:j + 1, i * BLOCK:(i + 1) * BLOCK]
                to = j * total_b + part * nb + i * BLOCK
                station = lax.broadcasted_iota(jnp.int32, (STATION_COUNT, BLOCK), 0)
                onehot[:, to:to + BLOCK] = jnp.where(station == which, 1.0, 0.0).astype(BF16)

    chi_acc[...] = jnp.zeros_like(chi_acc)
    pl.semaphore_wait(barrier, 2 * nch - 1 + peers)

    def swap_pair(count):
        return [
            send(g_stage.at[pl.ds(0, count)], own_t.at[pl.ds(0, count), here_rows, :],
                 ex_send.at[0], ex_recv.at[0], there(sib)),
            send(m_stage.at[pl.ds(0, count * 64)], m_all.at[pl.ds(0, count * 64), pl.ds(nb, nb)],
                 ex_send.at[2], ex_recv.at[2], there(sib)),
        ]

    give = {0: swap_pair(HELD), 1: swap_pair(1)}
    swaps = [
        send(s_all.at[0], s_all.at[1], ex_send.at[1], ex_recv.at[1], there(sib)),
        send(v_stage, v_all.at[:, pl.ds(nb, nb)], ex_send.at[3], ex_recv.at[3], there(sib)),
    ]

    def per_core(what):
        for which in range(2):
            @pl.when(core == which)
            def _():
                what(which)

    per_core(lambda which: [one.start() for one in give[which]] and None)
    for swap in swaps:
        swap.start()
    chip_rows = pl.ds(pl.multiple_of(chip * half, half), half)

    def ag_copy(c, k):
        return send(gains.at[c, chip_rows, :], gains.at[c, chip_rows, :],
                    ag_send.at[c], ag_recv.at[c], there(peer(k) * 2 + core))

    per_core(lambda which: give[1 - which][0].wait_recv())
    for c in range(HELD):
        def gather_start():
            gains[c, chip_rows, :] = jnp.transpose(own_t[c])
            for k in range(peers):
                ag_copy(c, k).start()

        mine(c, gather_start)
    hot(0)
    swaps[0].wait_recv()
    hot(1)
    per_core(lambda which: give[1 - which][1].wait_recv())
    swaps[1].wait_recv()
    per_core(lambda which: [one.wait_send() for one in give[which]] and None)
    for swap in swaps:
        swap.wait_send()

    def store_pair(c, row, cols, one, two):
        both = jnp.concatenate([one, two], axis=0)
        hi = both.astype(BF16)
        term[c, row:row + 16, cols] = hi
        term[c, 128 + row:144 + row, cols] = (both - hi.astype(F32)).astype(BF16)

    def terms(c, step):
        both = gains_hl[c]
        chi = jnp.zeros((1, lanes), F32)
        for i in range(total_b // BLOCK):
            cols = pl.ds(i * BLOCK, BLOCK)
            cols_q = pl.ds(total_b + i * BLOCK, BLOCK)
            gp = jnp.dot(both, onehot[:, cols], preferred_element_type=F32)
            gp = gp[:64] + gp[64:]
            gq = jnp.dot(both, onehot[:, cols_q], preferred_element_type=F32)
            gq = gq[:64] + gq[64:]

            def part(x):
                return pairs([x[8 * k:8 * k + 8] for k in range(8)])

            jp = part(gp)
            jq = part(gq)
            mod = pairs([m_all[c * 64 + 8 * k:c * 64 + 8 * k + 8, cols] for k in range(8)])
            y_one = matmul22(mod, herm(jq))
            pred = flat(matmul22(jp, y_one))
            y_two = matmul22(herm(mod), herm(jp))
            resid = []
            for k in range(8):
                one = v_all[c * 8 + k:c * 8 + k + 1, cols] - jnp.sum(pred[k], axis=0, keepdims=True)
                for j in range(0, BLOCK, lanes):
                    chi = chi + one[:, j:j + lanes] * one[:, j:j + lanes]
                resid.append(one)
            resid = pairs(resid)
            a_one = flat(matmul22(resid, herm(y_one))) + gram_parts(y_one)
            a_two = flat(matmul22(herm(resid), herm(y_two))) + gram_parts(y_two)
            for k in range(0, 12, 2):
                store_pair(c, 8 * k, cols, a_one[k], a_one[k + 1])
                store_pair(c, 8 * k, cols_q, a_two[k], a_two[k + 1])
        chi_acc[pl.ds(step, 1), :] += chi

    lane_a = lax.broadcasted_iota(jnp.int32, (side, lanes), 1)
    lane_b = lax.broadcasted_iota(jnp.int32, (quarter, lanes), 1)

    def rs_copy(c, k):
        return send(norm.at[c, peer(k)], recv.at[c, k], rs_send.at[c], rs_recv.at[c],
                    there(peer(k) * 2 + core))

    def scatter(c):
        sums = nt_dot(onehot[...], term[c])
        sums = sums[:, :lanes] + sums[:, lanes:]
        lower = sums[:side]
        upper = pltpu.roll(sums[side:], 64, 1)
        packed = jnp.where(lane_a < 64, lower, upper)
        for j in range(chips):
            norm[c, j, :half, :] = packed[j * half:(j + 1) * half]
            mid_row = j * half + quarter
            end = (j + 1) * half
            low_one = lower[j * half:mid_row]
            low_two = pltpu.roll(lower[mid_row:end], 32, 1)
            up_one = upper[j * half:mid_row]
            up_two = pltpu.roll(upper[mid_row:end], 32, 1)
            norm[c, j, half:size, :] = jnp.where(
                lane_b < 64,
                jnp.where(lane_b < 32, up_one, up_two),
                jnp.where(lane_b < 96, low_one, low_two))
        for k in range(peers):
            rs_copy(c, k).start()

    def rs_whole(c):
        return send(norm.at[c, pl.ds(0, peers)], recv.at[c], rs_send.at[c], rs_recv.at[c], there(sib))

    def ag_whole(c):
        part = gains.at[c, pl.ds(0, peers * half), :]
        return send(part, part, ag_send.at[c], ag_recv.at[c], there(sib))

    def solve(c):
        total = norm[c, chip]
        rs_whole(c).wait_recv()
        parts = [total] + [recv[c, k] for k in range(peers)]
        while len(parts) > 1:
            parts = [sum(parts[j + 1:j + 2], parts[j]) for j in range(0, len(parts), 2)]
        total = parts[0]
        r_t = jnp.transpose(total[:half])
        b_t = jnp.transpose(jnp.concatenate(
            [total[half:], pltpu.roll(total[half:], 96, 1)], axis=0))
        fresh_rows = []
        for h in range(2):
            old = [own_t[c, h * 64 + 8 * k:h * 64 + 8 * k + 8, :] for k in range(8)]
            amat = pairs([r_t[h * 64 + 8 * k:h * 64 + 8 * k + 8, :] - old[k] for k in range(8)])
            base = 64 * (1 - h)
            diag_one, diag_two, off_re, off_im = [
                b_t[base + 8 * k:base + 8 * k + 8, :] for k in range(4)]
            diag_one = diag_one + REG
            diag_two = diag_two + REG
            det = diag_one * diag_two - off_re * off_re - off_im * off_im
            scale = 0.5 / det
            d_one = diag_one * scale
            d_two = diag_two * scale
            o_re = off_re * scale
            o_im = off_im * scale
            for row in range(2):
                a0 = amat[2 * row]
                a1 = amat[2 * row + 1]
                n0 = cadd((a0[0] * d_two, a0[1] * d_two), cmul(a1, (-o_re, o_im)))
                n1 = cadd(cmul(a0, (-o_re, -o_im)), (a1[0] * d_one, a1[1] * d_one))
                k = 4 * row
                fresh_rows += [old[k] + n0[0], old[k + 1] + n0[1],
                               old[k + 2] + n1[0], old[k + 3] + n1[1]]
        fresh = jnp.concatenate(fresh_rows, axis=0)
        own_t[c] = fresh
        return jnp.transpose(fresh)

    def prepare(c):
        ag_whole(c).wait_recv()
        turned = jnp.transpose(gains[c])
        turned = jnp.concatenate([turned[:64], turned[64:]], axis=1)
        hi = turned.astype(BF16)
        gains_hl[c, :64] = hi
        gains_hl[c, 64:] = (turned - hi.astype(F32)).astype(BF16)

    def after_scatter(c):
        ag_whole(c).wait_send()

    def after_solve(c):
        rs_whole(c).wait_send()

    def early(step, carry):
        for c in range(HELD):
            def forth():
                prepare(c)
                terms(c, step)
                scatter(c)

            mine(c, forth)
        for c in range(HELD):
            def back():
                rows = solve(c)
                after_scatter(c)
                gains[c, chip_rows, :] = rows
                for k in range(peers):
                    ag_copy(c, k).start()
                after_solve(c)

            mine(c, back)
        return carry

    lax.fori_loop(0, ITERS - 1, early, 0)

    def xy_copy(k):
        return send(chi_acc, chi_xy.at[k], xy_send.at[0], xy_recv.at[0],
                    there(peer(k) * 2 + core))

    def z_copy(k):
        return send(chi_plane, chi_z.at[k - 1], z_send.at[0], z_recv.at[0], along_z(k))

    def up(c, which):
        g = core + c
        return send(fin.at[1, g], fin.at[0, g], fin_send.at[c, which],
                    fin_recv.at[0, g], there(chip * 2 + which, (z + 1) % nch))

    def down(c, which):
        g = core + c
        return send(fin.at[1, g], fin.at[2, g], fin_send.at[c, 2 + which],
                    fin_recv.at[2, g], there(chip * 2 + which, (z + nch - 1) % nch))

    def across(c):
        g = core + c
        return send(fin.at[1, g], fin.at[1, g], fin_send.at[c, 4],
                    fin_recv.at[1, g], there(sib))

    def halo(c):
        fin[1, core + c] = solve(c)
        after_scatter(c)

        @pl.when(z < nch - 1)
        def _():
            for which in range(2):
                up(c, which).start()

        @pl.when(z > 0)
        def _():
            for which in range(2):
                down(c, which).start()

        across(c).start()

    def xy_start():
        for k in range(peers):
            xy_copy(k).start()

    for c in range(HELD):
        def forth():
            prepare(c)
            terms(c, ITERS - 1)
            if c == 0:
                pl.when(core == 0)(xy_start)
            if c == HELD - 1:
                xy_start()
            scatter(c)

        mine(c, forth)

    @pl.when(z == 0)
    def _():
        fin[0] = jnp.zeros(fin.shape[1:], F32)

    @pl.when(z == nch - 1)
    def _():
        fin[2] = jnp.zeros(fin.shape[1:], F32)

    shape = (12 * half, 4 * lanes)
    row = lax.broadcasted_iota(jnp.int32, shape, 0)
    col = lax.broadcasted_iota(jnp.int32, shape, 1)
    to = col // lanes
    shift = row // half - 4 - to

    def weigh(step):
        step = step.astype(F32)
        return jnp.exp(-(step * step) / (2.0 * KERNEL_VAR))

    line = lax.broadcasted_iota(jnp.int32, (1, 4 * lanes), 1) // lanes
    denom = jnp.zeros((1, 4 * lanes), F32)
    for s in range(-SPAN, SPAN + 1):
        at = z * 4 + line + s
        denom = denom + jnp.where((at >= 0) & (at < 4 * nch), weigh(jnp.full((1, 4 * lanes), s, jnp.int32)), 0.0)
    mixing = jnp.where(
        (row % half == col % lanes) & (shift >= -SPAN) & (shift <= SPAN), weigh(shift) / denom, 0.0)

    def plane_chi():
        chi = chi_acc[...]
        send(chi_xy, chi_xy, xy_send.at[0], xy_recv.at[0], there(sib)).wait_recv()
        for k in range(peers):
            chi = chi + chi_xy[k]
        chi_plane[...] = chi
        for k in z_order:
            z_copy(k).start()

    halo(0)

    @pl.when(core == 1)
    def _():
        halo(1)

    plane_chi()

    @pl.when(core == 1)
    def _():
        halo(2)

    for c in range(HELD):
        mine(c, lambda: after_solve(c))

    def wait_fin(slot, which):
        for g in which:
            send(fin.at[slot, g], fin.at[slot, g], fin_send.at[0, 0],
                 fin_recv.at[slot, g], there(sib)).wait_recv()

    per_core(lambda which: wait_fin(1, range(1, 4) if which == 0 else range(1)))

    @pl.when(z > 0)
    def _():
        wait_fin(0, range(4))

    @pl.when(z < nch - 1)
    def _():
        wait_fin(2, range(4))

    slabs = jnp.transpose(fin[...].reshape(12 * half, lanes))
    slabs = jnp.where(core == 0, slabs[:64], slabs[64:])
    smooth = jnp.dot(slabs, mixing, precision=lax.Precision.HIGHEST, preferred_element_type=F32)
    for c in range(4):
        out_ref[c] = smooth[:, c * lanes:c * lanes + half]

    chi = chi_plane[...]
    send(chi_z, chi_z, z_send.at[0], z_recv.at[0], there(sib)).wait_recv()
    for k in z_order:
        chi = chi + chi_z[k - 1]
    chi_ref[...] = jnp.broadcast_to(jnp.sum(chi, axis=1, keepdims=True), (8, lanes))

    send(chi_xy, chi_xy, xy_send.at[0], xy_recv.at[0], there(sib)).wait_send()
    send(chi_z, chi_z, z_send.at[0], z_recv.at[0], there(sib)).wait_send()
    for c in range(HELD):
        def finish():
            across(c).wait_send()

            @pl.when(z < nch - 1)
            def _():
                for which in range(2):
                    up(c, which).wait_send()

            @pl.when(z > 0)
            def _():
                for which in range(2):
                    down(c, which).wait_send()

        mine(c, finish)


def on_device(visibilities, model, first_station, second_station, gain_offset):
    nb = visibilities.shape[2]
    half = gain_offset.shape[3]
    chips = lax.axis_size("bl") // 2
    nch = lax.axis_size("ch")
    size = half + half // 2
    total_b = 2 * nb
    peers = chips - 1
    vmem = pl.BlockSpec(memory_space=pltpu.VMEM)
    hbm = pl.BlockSpec(memory_space=pltpu.HBM)
    dma = pltpu.SemaphoreType.DMA
    smooth, chi = pl.pallas_call(
        functools.partial(kernel, chips, nch),
        out_shape=(
            jax.ShapeDtypeStruct((4, 64, half), F32),
            jax.ShapeDtypeStruct((8, 128), F32),
        ),
        in_specs=[hbm] * 5,
        out_specs=(vmem, vmem),
        scratch_shapes=[
            pltpu.VMEM(visibilities.shape, F32),
            pltpu.VMEM(model.shape, BF16),
            pltpu.VMEM((1, nb), jnp.int32),
            pltpu.VMEM((1, nb), jnp.int32),
            pltpu.VMEM(gain_offset.shape, F32),
            pltpu.VMEM((64 * HELD, total_b), F32),
            pltpu.VMEM((64 * HELD, nb), F32),
            pltpu.VMEM((8 * HELD, total_b), F32),
            pltpu.VMEM((8 * HELD, nb), F32),
            pltpu.VMEM((2, 8, nb), jnp.int32),
            pltpu.VMEM((HELD, 64, half), F32),
            pltpu.VMEM((STATION_COUNT, 2 * total_b), BF16),
            pltpu.VMEM((HELD, chips * half, 128), F32),
            pltpu.VMEM((HELD, 128, STATION_COUNT), BF16),
            pltpu.VMEM((HELD, 128, half), F32),
            pltpu.VMEM((HELD, 256, 2 * total_b), BF16),
            pltpu.VMEM((HELD, chips, size, 128), F32),
            pltpu.VMEM((HELD, peers, size, 128), F32),
            pltpu.VMEM((8, 128), F32),
            pltpu.VMEM((8, 128), F32),
            pltpu.VMEM((peers, 8, 128), F32),
            pltpu.VMEM((2 * nch - 1, 8, 128), F32),
            pltpu.VMEM((3, 4, half, 128), F32),
            dma((5,)),
            dma((4,)),
            dma((4,)),
            dma((HELD,)),
            dma((HELD,)),
            dma((HELD,)),
            dma((HELD,)),
            dma((HELD, 5)),
            dma((3, 4)),
            dma((1,)),
            dma((1,)),
            dma((1,)),
            dma((1,)),
        ],
        compiler_params=pltpu.CompilerParams(
            collective_id=0, has_side_effects=True, vmem_limit_bytes=48 * 1024 * 1024),
    )(*[pltpu.with_memory_space_constraint(x, pltpu.HBM) for x in (visibilities, model, first_station[None], second_station[None], gain_offset)])
    smoothed = jnp.transpose(smooth.reshape(4, 8, 8, half), (2, 1, 0, 3))
    count_vis = 8.0 * nb * lax.axis_size("bl") * 4 * nch
    misfit = chi[:ITERS, 0] / count_vis
    return (smoothed, misfit)


def solution(mesh):
    return jax.shard_map(
        on_device,
        mesh=mesh,
        in_specs=(
            P(None, "ch", "bl"),
            P(None, None, "ch", "bl"),
            P("bl"),
            P("bl"),
            P(None, None, "ch", "bl"),
        ),
        out_specs=(P(None, None, "ch", "bl"), P()),
        check_vma=False,
    )
```

```python
import functools

import jax
import jax.numpy as jnp
from jax import lax
from jax.experimental import pallas as pl
from jax.experimental.pallas import tpu as pltpu
from jax.sharding import PartitionSpec as P

STATION_COUNT = 512
ITERS = 3
SPAN = 4
REG = 1.0
KERNEL_VAR = 4.0
BLOCK = 256
HELD = 3
F32 = jnp.float32
BF16 = jnp.bfloat16


def cmul(a, b):
    return (a[0] * b[0] - a[1] * b[1], a[0] * b[1] + a[1] * b[0])


def cadd(a, b):
    return (a[0] + b[0], a[1] + b[1])


def conj(a):
    return (a[0], -a[1])


def matmul22(a, b):
    return [
        cadd(cmul(a[0], b[0]), cmul(a[1], b[2])),
        cadd(cmul(a[0], b[1]), cmul(a[1], b[3])),
        cadd(cmul(a[2], b[0]), cmul(a[3], b[2])),
        cadd(cmul(a[2], b[1]), cmul(a[3], b[3])),
    ]


def herm(a):
    return [conj(a[0]), conj(a[2]), conj(a[1]), conj(a[3])]


def gram_parts(y):
    diag_one = y[0][0] ** 2 + y[0][1] ** 2 + y[1][0] ** 2 + y[1][1] ** 2
    diag_two = y[2][0] ** 2 + y[2][1] ** 2 + y[3][0] ** 2 + y[3][1] ** 2
    off = cadd(cmul(y[0], conj(y[2])), cmul(y[1], conj(y[3])))
    return [diag_one, diag_two, off[0], off[1]]


def flat(m):
    return [m[k][j] for k in range(4) for j in range(2)]


def pairs(parts):
    return [(parts[2 * k], parts[2 * k + 1]) for k in range(4)]


def nt_dot(a, b):
    return lax.dot_general(a, b, (((1,), (1,)), ((), ())), preferred_element_type=F32)


def plane(chips):
    ny = 1
    while ny * ny < chips:
        ny *= 2
    return (chips // ny, ny)


def far_first(chips):
    nx, ny = plane(chips)

    def hops(o):
        return min(o[0], nx - o[0]) + min(o[1], ny - o[1])

    others = [(i, j) for i in range(nx) for j in range(ny) if i + j > 0]
    return sorted(others, key=lambda o: -hops(o))


def kernel(
    chips,
    nch,
    vis_hbm,
    model_hbm,
    first_hbm,
    second_hbm,
    goff_hbm,
    out_ref,
    chi_ref,
    vis_in,
    model_in,
    first_in,
    second_in,
    goff_in,
    m_all,
    m_stage,
    v_all,
    v_stage,
    s_all,
    g_stage,
    onehot,
    gains,
    gains_hl,
    own_t,
    term,
    norm,
    recv,
    chi_acc,
    chi_plane,
    chi_xy,
    chi_z,
    fin,
    in_sem,
    ex_send,
    ex_recv,
    rs_send,
    rs_recv,
    ag_send,
    ag_recv,
    fin_send,
    fin_recv,
    xy_send,
    xy_recv,
    z_send,
    z_recv,
):
    nb = vis_in.shape[2]
    total_b = 2 * nb
    half = goff_in.shape[3]
    quarter = half // 2
    side = chips * half
    size = half + quarter
    nx, ny = plane(chips)
    offsets = far_first(chips)
    peers = len(offsets)
    me = lax.axis_index("bl")
    z = lax.axis_index("ch")
    chip = me // 2
    core = me % 2
    sib = chip * 2 + (1 - core)
    px = chip // ny
    py = chip % ny
    lanes = 128

    def there(bl, ch=None):
        return {"bl": bl, "ch": z if ch is None else ch}

    def peer(k):
        return ((px + offsets[k][0]) % nx) * ny + (py + offsets[k][1]) % ny

    def send(src, dst, ssem, rsem, where):
        return pltpu.make_async_remote_copy(
            src_ref=src, dst_ref=dst, send_sem=ssem, recv_sem=rsem,
            device_id=where, device_id_type=pl.DeviceIdType.MESH)

    def along_z(k):
        return there(chip * 2 + (core + k) % 2, (z + k // 2) % nch)

    z_order = sorted(range(1, 2 * nch), key=lambda k: -min(k // 2, nch - k // 2))

    barrier = pltpu.get_barrier_semaphore()
    for k in z_order:
        pl.semaphore_signal(barrier, inc=1, device_id=along_z(k),
                            device_id_type=pl.DeviceIdType.MESH)
    for k in range(peers):
        pl.semaphore_signal(barrier, inc=1, device_id=there(peer(k) * 2 + core),
                            device_id_type=pl.DeviceIdType.MESH)

    loads = [
        pltpu.make_async_copy(goff_hbm, goff_in, in_sem.at[0]),
        pltpu.make_async_copy(model_hbm, model_in, in_sem.at[1]),
        pltpu.make_async_copy(vis_hbm, vis_in, in_sem.at[2]),
        pltpu.make_async_copy(first_hbm, first_in, in_sem.at[3]),
        pltpu.make_async_copy(second_hbm, second_in, in_sem.at[4]),
    ]
    for load in loads:
        load.start()

    def mine(c, work):
        if c == 0:
            work()
        else:
            pl.when(core == 1)(work)

    r = lax.broadcasted_iota(jnp.int32, (256, 256), 0)
    q = lax.broadcasted_iota(jnp.int32, (256, 256), 1)
    chan = (r // 64 + core) % 4
    perm = jnp.where(q == (r % 8) * 32 + ((r // 8) % 8) * 4 + chan, 1.0, 0.0).astype(BF16)

    loads[0].wait()
    offs = goff_in[...].reshape(256, half)
    hi = offs.astype(BF16)
    rest = offs - hi.astype(F32)
    mid = rest.astype(BF16)
    low = (rest - mid.astype(F32)).astype(BF16)
    turned = [jnp.dot(perm, one, preferred_element_type=F32) for one in (hi, mid, low)]
    comp = (lax.broadcasted_iota(jnp.int32, (256, half), 0) // 8) % 8
    start = jnp.where((comp == 0) | (comp == 6), 1.0, 0.0) + ((turned[0] + turned[1]) + turned[2])
    here_rows = pl.ds(pl.multiple_of(core * 64, 64), 64)
    for c in range(HELD):
        own_t[c, here_rows, :] = start[c * 64:c * 64 + 64]

    @pl.when(core == 0)
    def _():
        for c in range(HELD):
            g_stage[c] = start[(c + 1) * 64:(c + 2) * 64]

    @pl.when(core == 1)
    def _():
        g_stage[0] = start[192:]

    loads[1].wait()
    permuted = jnp.dot(perm, model_in[...].reshape(256, nb), preferred_element_type=F32)
    m_all[:, :nb] = permuted[:192]

    @pl.when(core == 0)
    def _():
        m_stage[...] = permuted[64:]

    @pl.when(core == 1)
    def _():
        m_stage[:64] = permuted[192:]

    loads[2].wait()
    for c in range(HELD):
        for k in range(8):
            row = c * 8 + k
            v_all[row:row + 1, :nb] = vis_in[k, pl.ds(core + c, 1), :]
            v_stage[row:row + 1, :] = vis_in[k, pl.ds(1 - core + c, 1), :]
    loads[3].wait()
    loads[4].wait()

    def place(s):
        rem = s % (2 * half)
        return (rem // half) * side + (s // (2 * half)) * half + rem % half

    s_all[0, 0:1, :] = place(first_in[...])
    s_all[0, 1:2, :] = place(second_in[...])
    s_all[0, 2:8, :] = jnp.zeros((6, nb), jnp.int32)

    def hot(part):
        for i in range(nb // BLOCK):
            for j in range(2):
                which = s_all[part, j:j + 1, i * BLOCK:(i + 1) * BLOCK]
                to = j * total_b + part * nb + i * BLOCK
                station = lax.broadcasted_iota(jnp.int32, (STATION_COUNT, BLOCK), 0)
                onehot[:, to:to + BLOCK] = jnp.where(station == which, 1.0, 0.0).astype(BF16)

    chi_acc[...] = jnp.zeros_like(chi_acc)
    pl.semaphore_wait(barrier, 2 * nch - 1 + peers)

    def swap_pair(count):
        return [
            send(g_stage.at[pl.ds(0, count)], own_t.at[pl.ds(0, count), here_rows, :],
                 ex_send.at[0], ex_recv.at[0], there(sib)),
            send(m_stage.at[pl.ds(0, count * 64)], m_all.at[pl.ds(0, count * 64), pl.ds(nb, nb)],
                 ex_send.at[2], ex_recv.at[2], there(sib)),
        ]

    give = {0: swap_pair(HELD), 1: swap_pair(1)}
    swaps = [
        send(s_all.at[0], s_all.at[1], ex_send.at[1], ex_recv.at[1], there(sib)),
        send(v_stage, v_all.at[:, pl.ds(nb, nb)], ex_send.at[3], ex_recv.at[3], there(sib)),
    ]

    def per_core(what):
        for which in range(2):
            @pl.when(core == which)
            def _():
                what(which)

    per_core(lambda which: [one.start() for one in give[which]] and None)
    for swap in swaps:
        swap.start()
    chip_rows = pl.ds(pl.multiple_of(chip * half, half), half)

    def ag_copy(c, k):
        return send(gains.at[c, chip_rows, :], gains.at[c, chip_rows, :],
                    ag_send.at[c], ag_recv.at[c], there(peer(k) * 2 + core))

    per_core(lambda which: give[1 - which][0].wait_recv())
    for c in range(HELD):
        def gather_start():
            gains[c, chip_rows, :] = jnp.transpose(own_t[c])
            for k in range(peers):
                ag_copy(c, k).start()

        mine(c, gather_start)
    hot(0)
    swaps[0].wait_recv()
    hot(1)
    per_core(lambda which: give[1 - which][1].wait_recv())
    swaps[1].wait_recv()
    per_core(lambda which: [one.wait_send() for one in give[which]] and None)
    for swap in swaps:
        swap.wait_send()

    def store_pair(c, row, cols, one, two):
        both = jnp.concatenate([one, two], axis=0)
        hi = both.astype(BF16)
        term[c, row:row + 16, cols] = hi
        term[c, 128 + row:144 + row, cols] = (both - hi.astype(F32)).astype(BF16)

    def terms(c, step):
        both = gains_hl[c]
        chi = jnp.zeros((1, lanes), F32)
        def body(i, chi):
            cols = pl.ds(pl.multiple_of(i * BLOCK, BLOCK), BLOCK)
            cols_q = pl.ds(pl.multiple_of(total_b + i * BLOCK, BLOCK), BLOCK)
            gp = jnp.dot(both, onehot[:, cols], preferred_element_type=F32)
            gp = gp[:64] + gp[64:]
            gq = jnp.dot(both, onehot[:, cols_q], preferred_element_type=F32)
            gq = gq[:64] + gq[64:]

            def part(x):
                return pairs([x[8 * k:8 * k + 8] for k in range(8)])

            jp = part(gp)
            jq = part(gq)
            mod = pairs([m_all[c * 64 + 8 * k:c * 64 + 8 * k + 8, cols] for k in range(8)])
            y_one = matmul22(mod, herm(jq))
            pred = flat(matmul22(jp, y_one))
            y_two = matmul22(herm(mod), herm(jp))
            resid = []
            for k in range(8):
                one = v_all[c * 8 + k:c * 8 + k + 1, cols] - jnp.sum(pred[k], axis=0, keepdims=True)
                for j in range(0, BLOCK, lanes):
                    chi = chi + one[:, j:j + lanes] * one[:, j:j + lanes]
                resid.append(one)
            resid = pairs(resid)
            a_one = flat(matmul22(resid, herm(y_one))) + gram_parts(y_one)
            a_two = flat(matmul22(herm(resid), herm(y_two))) + gram_parts(y_two)
            for k in range(0, 12, 2):
                store_pair(c, 8 * k, cols, a_one[k], a_one[k + 1])
                store_pair(c, 8 * k, cols_q, a_two[k], a_two[k + 1])
            return chi

        chi = lax.fori_loop(0, total_b // BLOCK, body, chi, unroll=2)
        chi_acc[pl.ds(step, 1), :] += chi

    lane_a = lax.broadcasted_iota(jnp.int32, (side, lanes), 1)
    lane_b = lax.broadcasted_iota(jnp.int32, (quarter, lanes), 1)

    def rs_copy(c, k):
        return send(norm.at[c, peer(k)], recv.at[c, k], rs_send.at[c], rs_recv.at[c],
                    there(peer(k) * 2 + core))

    def scatter(c):
        sums = nt_dot(onehot[...], term[c])
        sums = sums[:, :lanes] + sums[:, lanes:]
        lower = sums[:side]
        upper = pltpu.roll(sums[side:], 64, 1)
        packed = jnp.where(lane_a < 64, lower, upper)
        for j in range(chips):
            norm[c, j, :half, :] = packed[j * half:(j + 1) * half]
            mid_row = j * half + quarter
            end = (j + 1) * half
            low_one = lower[j * half:mid_row]
            low_two = pltpu.roll(lower[mid_row:end], 32, 1)
            up_one = upper[j * half:mid_row]
            up_two = pltpu.roll(upper[mid_row:end], 32, 1)
            norm[c, j, half:size, :] = jnp.where(
                lane_b < 64,
                jnp.where(lane_b < 32, up_one, up_two),
                jnp.where(lane_b < 96, low_one, low_two))
        for k in range(peers):
            rs_copy(c, k).start()

    def rs_whole(c):
        return send(norm.at[c, pl.ds(0, peers)], recv.at[c], rs_send.at[c], rs_recv.at[c], there(sib))

    def ag_whole(c):
        part = gains.at[c, pl.ds(0, peers * half), :]
        return send(part, part, ag_send.at[c], ag_recv.at[c], there(sib))

    def solve(c):
        total = norm[c, chip]
        rs_whole(c).wait_recv()
        for k in range(peers):
            total = total + recv[c, k]
        r_t = jnp.transpose(total[:half])
        b_t = jnp.transpose(jnp.concatenate(
            [total[half:], pltpu.roll(total[half:], 96, 1)], axis=0))
        fresh_rows = []
        for h in range(2):
            old = [own_t[c, h * 64 + 8 * k:h * 64 + 8 * k + 8, :] for k in range(8)]
            amat = pairs([r_t[h * 64 + 8 * k:h * 64 + 8 * k + 8, :] - old[k] for k in range(8)])
            base = 64 * (1 - h)
            diag_one, diag_two, off_re, off_im = [
                b_t[base + 8 * k:base + 8 * k + 8, :] for k in range(4)]
            diag_one = diag_one + REG
            diag_two = diag_two + REG
            det = diag_one * diag_two - off_re * off_re - off_im * off_im
            scale = 0.5 / det
            d_one = diag_one * scale
            d_two = diag_two * scale
            o_re = off_re * scale
            o_im = off_im * scale
            for row in range(2):
                a0 = amat[2 * row]
                a1 = amat[2 * row + 1]
                n0 = cadd((a0[0] * d_two, a0[1] * d_two), cmul(a1, (-o_re, o_im)))
                n1 = cadd(cmul(a0, (-o_re, -o_im)), (a1[0] * d_one, a1[1] * d_one))
                k = 4 * row
                fresh_rows += [old[k] + n0[0], old[k + 1] + n0[1],
                               old[k + 2] + n1[0], old[k + 3] + n1[1]]
        fresh = jnp.concatenate(fresh_rows, axis=0)
        own_t[c] = fresh
        return jnp.transpose(fresh)

    def prepare(c):
        ag_whole(c).wait_recv()
        turned = jnp.transpose(gains[c])
        turned = jnp.concatenate([turned[:64], turned[64:]], axis=1)
        hi = turned.astype(BF16)
        gains_hl[c, :64] = hi
        gains_hl[c, 64:] = (turned - hi.astype(F32)).astype(BF16)

    def after_scatter(c):
        ag_whole(c).wait_send()

    def after_solve(c):
        rs_whole(c).wait_send()

    def early(step, carry):
        for c in range(HELD):
            def forth():
                prepare(c)
                terms(c, step)
                scatter(c)
                after_scatter(c)

            mine(c, forth)
        for c in range(HELD):
            def back():
                gains[c, chip_rows, :] = solve(c)
                for k in range(peers):
                    ag_copy(c, k).start()
                after_solve(c)

            mine(c, back)
        return carry

    lax.fori_loop(0, ITERS - 1, early, 0)

    def xy_copy(k):
        return send(chi_acc, chi_xy.at[k], xy_send.at[0], xy_recv.at[0],
                    there(peer(k) * 2 + core))

    def z_copy(k):
        return send(chi_plane, chi_z.at[k - 1], z_send.at[0], z_recv.at[0], along_z(k))

    def up(c, which):
        g = core + c
        return send(fin.at[1, g], fin.at[0, g], fin_send.at[c, which],
                    fin_recv.at[0, g], there(chip * 2 + which, (z + 1) % nch))

    def down(c, which):
        g = core + c
        return send(fin.at[1, g], fin.at[2, g], fin_send.at[c, 2 + which],
                    fin_recv.at[2, g], there(chip * 2 + which, (z + nch - 1) % nch))

    def across(c):
        g = core + c
        return send(fin.at[1, g], fin.at[1, g], fin_send.at[c, 4],
                    fin_recv.at[1, g], there(sib))

    def halo(c):
        fin[1, core + c] = solve(c)

        @pl.when(z < nch - 1)
        def _():
            for which in range(2):
                up(c, which).start()

        @pl.when(z > 0)
        def _():
            for which in range(2):
                down(c, which).start()

        across(c).start()

    def xy_start():
        for k in range(peers):
            xy_copy(k).start()

    for c in range(HELD):
        def forth():
            prepare(c)
            terms(c, ITERS - 1)
            if c == 0:
                pl.when(core == 0)(xy_start)
            if c == HELD - 1:
                xy_start()
            scatter(c)
            after_scatter(c)

        mine(c, forth)

    @pl.when(z == 0)
    def _():
        fin[0] = jnp.zeros(fin.shape[1:], F32)

    @pl.when(z == nch - 1)
    def _():
        fin[2] = jnp.zeros(fin.shape[1:], F32)

    shape = (12 * half, 4 * lanes)
    row = lax.broadcasted_iota(jnp.int32, shape, 0)
    col = lax.broadcasted_iota(jnp.int32, shape, 1)
    to = col // lanes
    shift = row // half - 4 - to

    def weigh(step):
        step = step.astype(F32)
        return jnp.exp(-(step * step) / (2.0 * KERNEL_VAR))

    line = lax.broadcasted_iota(jnp.int32, (1, 4 * lanes), 1) // lanes
    denom = jnp.zeros((1, 4 * lanes), F32)
    for s in range(-SPAN, SPAN + 1):
        at = z * 4 + line + s
        denom = denom + jnp.where((at >= 0) & (at < 4 * nch), weigh(jnp.full((1, 4 * lanes), s, jnp.int32)), 0.0)
    mixing = jnp.where(
        (row % half == col % lanes) & (shift >= -SPAN) & (shift <= SPAN), weigh(shift) / denom, 0.0)

    def plane_chi():
        chi = chi_acc[...]
        send(chi_xy, chi_xy, xy_send.at[0], xy_recv.at[0], there(sib)).wait_recv()
        for k in range(peers):
            chi = chi + chi_xy[k]
        chi_plane[...] = chi
        for k in z_order:
            z_copy(k).start()

    halo(0)

    @pl.when(core == 1)
    def _():
        halo(1)

    plane_chi()

    @pl.when(core == 1)
    def _():
        halo(2)

    for c in range(HELD):
        mine(c, lambda: after_solve(c))

    def wait_fin(slot, which):
        for g in which:
            send(fin.at[slot, g], fin.at[slot, g], fin_send.at[0, 0],
                 fin_recv.at[slot, g], there(sib)).wait_recv()

    per_core(lambda which: wait_fin(1, range(1, 4) if which == 0 else range(1)))

    @pl.when(z > 0)
    def _():
        wait_fin(0, range(4))

    @pl.when(z < nch - 1)
    def _():
        wait_fin(2, range(4))

    slabs = jnp.transpose(fin[...].reshape(12 * half, lanes))
    slabs = jnp.where(core == 0, slabs[:64], slabs[64:])
    smooth = jnp.dot(slabs, mixing, precision=lax.Precision.HIGHEST, preferred_element_type=F32)
    for c in range(4):
        out_ref[c] = smooth[:, c * lanes:c * lanes + half]

    chi = chi_plane[...]
    send(chi_z, chi_z, z_send.at[0], z_recv.at[0], there(sib)).wait_recv()
    for k in z_order:
        chi = chi + chi_z[k - 1]
    chi_ref[...] = jnp.broadcast_to(jnp.sum(chi, axis=1, keepdims=True), (8, lanes))

    send(chi_xy, chi_xy, xy_send.at[0], xy_recv.at[0], there(sib)).wait_send()
    send(chi_z, chi_z, z_send.at[0], z_recv.at[0], there(sib)).wait_send()
    for c in range(HELD):
        def finish():
            across(c).wait_send()

            @pl.when(z < nch - 1)
            def _():
                for which in range(2):
                    up(c, which).wait_send()

            @pl.when(z > 0)
            def _():
                for which in range(2):
                    down(c, which).wait_send()

        mine(c, finish)


def on_device(visibilities, model, first_station, second_station, gain_offset):
    nb = visibilities.shape[2]
    half = gain_offset.shape[3]
    chips = lax.axis_size("bl") // 2
    nch = lax.axis_size("ch")
    size = half + half // 2
    total_b = 2 * nb
    peers = chips - 1
    vmem = pl.BlockSpec(memory_space=pltpu.VMEM)
    hbm = pl.BlockSpec(memory_space=pltpu.HBM)
    dma = pltpu.SemaphoreType.DMA
    smooth, chi = pl.pallas_call(
        functools.partial(kernel, chips, nch),
        out_shape=(
            jax.ShapeDtypeStruct((4, 64, half), F32),
            jax.ShapeDtypeStruct((8, 128), F32),
        ),
        in_specs=[hbm] * 5,
        out_specs=(vmem, vmem),
        scratch_shapes=[
            pltpu.VMEM(visibilities.shape, F32),
            pltpu.VMEM(model.shape, BF16),
            pltpu.VMEM((1, nb), jnp.int32),
            pltpu.VMEM((1, nb), jnp.int32),
            pltpu.VMEM(gain_offset.shape, F32),
            pltpu.VMEM((64 * HELD, total_b), F32),
            pltpu.VMEM((64 * HELD, nb), F32),
            pltpu.VMEM((8 * HELD, total_b), F32),
            pltpu.VMEM((8 * HELD, nb), F32),
            pltpu.VMEM((2, 8, nb), jnp.int32),
            pltpu.VMEM((HELD, 64, half), F32),
            pltpu.VMEM((STATION_COUNT, 2 * total_b), BF16),
            pltpu.VMEM((HELD, chips * half, 128), F32),
            pltpu.VMEM((HELD, 128, STATION_COUNT), BF16),
            pltpu.VMEM((HELD, 128, half), F32),
            pltpu.VMEM((HELD, 256, 2 * total_b), BF16),
            pltpu.VMEM((HELD, chips, size, 128), F32),
            pltpu.VMEM((HELD, peers, size, 128), F32),
            pltpu.VMEM((8, 128), F32),
            pltpu.VMEM((8, 128), F32),
            pltpu.VMEM((peers, 8, 128), F32),
            pltpu.VMEM((2 * nch - 1, 8, 128), F32),
            pltpu.VMEM((3, 4, half, 128), F32),
            dma((5,)),
            dma((4,)),
            dma((4,)),
            dma((HELD,)),
            dma((HELD,)),
            dma((HELD,)),
            dma((HELD,)),
            dma((HELD, 5)),
            dma((3, 4)),
            dma((1,)),
            dma((1,)),
            dma((1,)),
            dma((1,)),
        ],
        compiler_params=pltpu.CompilerParams(
            collective_id=0, has_side_effects=True, vmem_limit_bytes=48 * 1024 * 1024),
    )(*[pltpu.with_memory_space_constraint(x, pltpu.HBM) for x in (visibilities, model, first_station[None], second_station[None], gain_offset)])
    smoothed = jnp.transpose(smooth.reshape(4, 8, 8, half), (2, 1, 0, 3))
    count_vis = 8.0 * nb * lax.axis_size("bl") * 4 * nch
    misfit = chi[:ITERS, 0] / count_vis
    return (smoothed, misfit)


def solution(mesh):
    return jax.shard_map(
        on_device,
        mesh=mesh,
        in_specs=(
            P(None, "ch", "bl"),
            P(None, None, "ch", "bl"),
            P("bl"),
            P("bl"),
            P(None, None, "ch", "bl"),
        ),
        out_specs=(P(None, None, "ch", "bl"), P()),
        check_vma=False,
    )
```
